256 devices in a mesh: seq: 128 (over x_lo, z, y, core), batch: 2 (over x_hi).
Axes of the slice: x: 4 (x_hi: 2, x_lo: 2; x = x_hi * 2 + x_lo), y: 4, z: 8, core: 2. Of those that a mesh axis runs over, the one named last changes fastest.
Arguments:
- queries: bfloat16 [8192, 1024], P(('batch', 'seq')), parts along dimension 0, may hold values from -8 to 8
- keys: bfloat16 [8192, 1024], P(('batch', 'seq')), parts along dimension 0, may hold values from -8 to 8
- values: bfloat16 [8192, 1024], P(('batch', 'seq')), parts along dimension 0, may hold values from -6 to 6
- cross_queries: bfloat16 [8192, 1024], P(('batch', 'seq')), parts along dimension 0, may hold values from -8 to 8
- text_states: bfloat16 [256, 128, 4096], P(('batch', 'seq')), parts along dimension 0, may hold values from -6 to 6
- cross_kv_weight: bfloat16 [4096, 2048], P('seq'), may hold values from -1 to 1
- owner: int32 [2], P('batch'), parts along dimension 0, may hold values from 0 to 127
- prompt_len: int32 [2], P('batch'), parts along dimension 0, may hold values from 16 to 128
Outputs:
- mixed: bfloat16 [8192, 1024], P(('batch', 'seq')), parts along dimension 0
The draws below stay inside these ranges and needn't reach their ends.
There are 2 independent parts, one for each index of `batch`. The reference program is written for one: setup_inputs(seed, part) draws one part's arguments, and reference() takes and returns one part's arrays. A program takes and returns all parts, laid end to end along the dimension named above; an argument that names none is the same for every part. Nothing has to cross between parts.
Inputs may be any that keep to these rules, and one draw needn't show every extreme that they name: The owner is one seq index of the sample. `prompt_len`: at least one prompt token is valid.
All inputs are finite; a program needn't handle non-finite values.
Results may differ from the reference program's by a relative error of at most 0.0076.
Values may be sent and summed in bfloat16 or wider, within the bound.
A program may use at most 128 MiB of HBM per device.

```python
import math
import jax
import jax.numpy as jnp
from jax import lax

HEAD_DIM = 128
HEADS = 8
TEXT_D = 4096
PROMPT = 128
INNER = 1024
TOKENS = 4096
N_SEQ = 128


def draw_queries(key, part):
    key = jax.random.fold_in(key, 1)
    drawn = jnp.clip(1.5 * jax.random.normal(key, (TOKENS, INNER), dtype=jnp.float32), -8.0, 8.0)
    return drawn.astype(jnp.bfloat16)


def draw_keys(key, part):
    key = jax.random.fold_in(key, 2)
    drawn = jnp.clip(1.5 * jax.random.normal(key, (TOKENS, INNER), dtype=jnp.float32), -8.0, 8.0)
    return drawn.astype(jnp.bfloat16)


def draw_cross_queries(key, part):
    key = jax.random.fold_in(key, 4)
    drawn = jnp.clip(1.5 * jax.random.normal(key, (TOKENS, INNER), dtype=jnp.float32), -8.0, 8.0)
    return drawn.astype(jnp.bfloat16)


def draw_text_states(key, part):
    key = jax.random.fold_in(key, 3)
    drawn = jnp.clip(jax.random.normal(key, (N_SEQ, PROMPT, TEXT_D), dtype=jnp.float32), -6.0, 6.0)
    return drawn.astype(jnp.bfloat16)


def draw_cross_kv_weight(key, part):
    key = jax.random.fold_in(key, 5)
    spread = 1.0 / math.sqrt(TEXT_D)
    drawn = jnp.clip(spread * jax.random.normal(key, (TEXT_D, 2 * INNER), dtype=jnp.float32), -6.0 * spread, 6.0 * spread)
    return drawn.astype(jnp.bfloat16)


def shard_levels(own_key, extent, pieces, smallest, high):
    def one(axis_at, shards_of):
        steps = jax.random.uniform(jax.random.fold_in(jax.random.fold_in(own_key, 6), axis_at), (shards_of,), jnp.float32, smallest / len(pieces), high / len(pieces))
        return jnp.repeat(jnp.exp(steps), extent[axis_at] // shards_of).reshape((-1,) + (1,) * (len(extent) - axis_at - 1))

    level = one(*pieces[0])
    for cut in pieces[1:]:
        level = level * one(*cut)
    return level


def normal_values(own_key, dims, scale, most, pieces=(), held_as=jnp.bfloat16):
    factor_of = shard_levels(own_key, dims, pieces, -0.22, 0.18) if pieces else 1.0
    values = jax.random.normal(own_key, dims, jnp.float32) * scale * factor_of
    return jnp.minimum(jnp.maximum(values, -most), most).astype(held_as)


def setup_inputs(seed: int = 0, part: int = 0) -> dict:
    splits = jax.random.split(jax.random.key(seed), 9)
    part_keys = jax.random.split(jax.random.fold_in(splits[8], part), 9)
    queries = draw_queries(jax.random.fold_in(jax.random.fold_in(splits[8], part), 71), part)
    keys = draw_keys(jax.random.fold_in(jax.random.fold_in(splits[8], part), 71), part)
    values = normal_values(part_keys[2], (TOKENS, INNER), 1.0, 6.0, ((0, 128),))
    cross_queries = draw_cross_queries(jax.random.fold_in(jax.random.fold_in(splits[8], part), 71), part)
    text_states = draw_text_states(jax.random.fold_in(jax.random.fold_in(splits[8], part), 71), part)
    cross_kv_weight = draw_cross_kv_weight(jax.random.fold_in(splits[8], 71), part)
    owner = jax.random.randint(part_keys[6], (1,), 0, N_SEQ).astype(jnp.int32)
    prompt_len = jax.random.randint(part_keys[7], (1,), PROMPT // 8, PROMPT + 1).astype(jnp.int32)
    return dict(queries=queries, keys=keys, values=values, cross_queries=cross_queries, text_states=text_states, cross_kv_weight=cross_kv_weight, owner=owner, prompt_len=prompt_len)


def attend(query_rows, key_rows, value_rows, valid):
    score_scale = 1.0 / math.sqrt(HEAD_DIM)
    query_count = query_rows.shape[0]
    key_count = key_rows.shape[0]
    query_heads = query_rows.reshape(query_count, HEADS, HEAD_DIM).transpose(1, 0, 2)
    key_heads = key_rows.reshape(key_count, HEADS, HEAD_DIM).transpose(1, 0, 2)
    value_heads = value_rows.reshape(key_count, HEADS, HEAD_DIM).transpose(1, 0, 2)

    def one_head(triple):
        head_query, head_key, head_value = triple
        scores = jnp.dot(head_query, head_key.T, preferred_element_type=jnp.float32) * score_scale
        scores = jnp.where(valid[None, :], scores, -1e+30)
        top_score = lax.optimization_barrier(jnp.max(scores, axis=1, keepdims=True))
        weights = jnp.exp(scores - top_score)
        total = lax.optimization_barrier(jnp.sum(weights, axis=1, keepdims=True))
        summed = jnp.dot(weights.astype(jnp.bfloat16), head_value, preferred_element_type=jnp.float32)
        return summed / total
    outputs = lax.map(one_head, (query_heads, key_heads, value_heads))
    return outputs.transpose(1, 0, 2).reshape(query_count, HEADS * HEAD_DIM)

def reference(queries, keys, values, cross_queries, text_states, cross_kv_weight, owner, prompt_len):
    all_valid = jnp.ones((keys.shape[0],), dtype=bool)
    self_out = attend(queries, keys, values, all_valid)
    prompt = lax.dynamic_index_in_dim(text_states, owner[0].astype(jnp.int32), 0, keepdims=False)
    cross_kv = jnp.dot(prompt, cross_kv_weight, preferred_element_type=jnp.float32).astype(jnp.bfloat16)
    inner = HEADS * HEAD_DIM
    prompt_valid = jnp.arange(PROMPT, dtype=jnp.int32) < prompt_len[0]
    cross_out = attend(cross_queries, cross_kv[:, :inner], cross_kv[:, inner:], prompt_valid)
    return (self_out + cross_out).astype(jnp.bfloat16)
```

```python
import math

import jax
import jax.numpy as jnp
from jax import lax
from jax.experimental import pallas as pl
from jax.experimental.pallas import tpu as pltpu
from jax.sharding import PartitionSpec as P

HEAD_DIM = 128
HEADS = 8
NX, NZ, NY, NC = 2, 8, 4, 2
PLANE = NX * NY
TOK = 32
SLOT = TOK * NZ
SCALE = 1.0 / math.sqrt(HEAD_DIM)
F32 = jnp.float32
BF16 = jnp.bfloat16


def index_of(x, z, y, core):
    return ((x * NZ + z) * NY + y) * NC + core


def send(src, dst, send_sem, recv_sem, x, z, y, core):
    pltpu.make_async_remote_copy(
        src_ref=src,
        dst_ref=dst,
        send_sem=send_sem,
        recv_sem=recv_sem,
        device_id={"seq": index_of(x, z, y, core)},
        device_id_type=pl.DeviceIdType.MESH,
    ).start()


def local(src, dst, sem):
    pltpu.make_async_copy(src, dst, sem).start()


def wait_bytes(ref, sem):
    pltpu.make_async_copy(ref, ref, sem).wait()


def head_columns(head):
    return pl.ds(pl.multiple_of(head * HEAD_DIM, HEAD_DIM), HEAD_DIM)


def rows(start, count):
    return pl.ds(pl.multiple_of(start, count), count)


def dot_last(a, b):
    return lax.dot_general(a, b, (((1,), (1,)), ((), ())), preferred_element_type=F32)


def dot_first(a, b):
    return lax.dot_general(a, b, (((0,), (0,)), ((), ())), preferred_element_type=F32)


def kernel(
    owner_ref,
    len_ref,
    q_hbm,
    k_hbm,
    v_hbm,
    cq_hbm,
    text_hbm,
    w_hbm,
    out_ref,
    slots,
    piece_out,
    pieces,
    sub_out,
    subs,
    sub_mine,
    prompt,
    weight,
    kv,
    queries,
    cross_q,
    part_out,
    parts,
    row_mine,
    cross_kv,
    acc_out,
    accs,
    stat_out,
    stats,
    out_rows,
    ss,
    rs,
    kv_rs,
    acc_rs,
    stat_rs,
):
    me = lax.axis_index("seq")
    core = me % NC
    y = (me // NC) % NY
    z = (me // (NC * NY)) % NZ
    x = me // (NC * NY * NZ)
    f = x * NY + y
    xc = x * NC + core
    other = 1 - core

    local(text_hbm.at[0, rows(core * 64, 64), :], slots.at[core], rs.at[0])
    local(k_hbm.at[:, head_columns(z)], kv.at[y, 0, rows(z * TOK, TOK), :], rs.at[1])
    local(v_hbm.at[:, head_columns(z)], kv.at[y, 1, rows(z * TOK, TOK), :], rs.at[1])
    local(q_hbm.at[:, head_columns(z)], queries.at[xc, rows(z * TOK, TOK), :], rs.at[2])
    local(cq_hbm.at[:, head_columns(z)], cross_q.at[rows(z * TOK, TOK), :], rs.at[3])
    my_weight = rows((z * NC + core) * TOK, TOK)
    local(w_hbm.at[:, head_columns(core * HEADS + z)], weight.at[my_weight, :], rs.at[4])

    barrier = pltpu.get_barrier_semaphore()

    def greet_line(t, carry):
        p = (z * NC + core + t) % (NZ * NC)
        pl.semaphore_signal(
            barrier, inc=1, device_id={"seq": index_of(x, p // NC, y, p % NC)}, device_id_type=pl.DeviceIdType.MESH
        )
        return carry

    def greet_plane(t, carry):
        p = (f + t) % PLANE
        for c in range(NC):
            pl.semaphore_signal(
                barrier, inc=1, device_id={"seq": index_of(p // NY, z, p % NY, c)}, device_id_type=pl.DeviceIdType.MESH
            )
        return carry

    lax.fori_loop(1, NZ * NC, greet_line, 0)
    lax.fori_loop(1, PLANE, greet_plane, 0)
    pl.semaphore_wait(barrier, NZ * NC - 1 + (PLANE - 1) * NC)

    send(text_hbm.at[0, rows(other * 64, 64), :], slots.at[core], ss.at[0], rs.at[0], x, z, y, other)

    def line_kv(t, carry):
        zz = (z + t) % NZ
        send(k_hbm.at[:, head_columns(zz)], kv.at[y, 0, rows(z * TOK, TOK), :], ss.at[1], rs.at[1], x, zz, y, core)
        send(v_hbm.at[:, head_columns(zz)], kv.at[y, 1, rows(z * TOK, TOK), :], ss.at[1], rs.at[1], x, zz, y, core)
        return carry

    def line_q(t, carry):
        zz = (z + t) % NZ
        send(q_hbm.at[:, head_columns(zz)], queries.at[xc, rows(z * TOK, TOK), :], ss.at[2], rs.at[2], x, zz, y, core)
        return carry

    def line_cq(t, carry):
        zz = (z + t) % NZ
        send(cq_hbm.at[:, head_columns(zz)], cross_q.at[rows(z * TOK, TOK), :], ss.at[3], rs.at[3], x, zz, y, core)
        return carry

    def line_w(t, carry):
        p = (z * NC + core + t) % (NZ * NC)
        zz, cc = p // NC, p % NC
        send(w_hbm.at[:, head_columns(cc * HEADS + zz)], weight.at[my_weight, :], ss.at[4], rs.at[4], x, zz, y, cc)
        return carry

    lax.fori_loop(1, NZ, line_kv, 0)
    lax.fori_loop(1, NZ, line_q, 0)

    owner = owner_ref[0]
    wait_bytes(slots, rs.at[0])
    for fx in range(NX):
        for yp in range(NY // 2):
            for zp in range(NZ // 2):
                base = fx * (NZ * 256) + zp * 512 + yp * 128
                a = slots[owner % NC, :, base : base + 128]
                b = slots[owner % NC, :, base + 256 : base + 384]
                piece_out[fx * NY + 2 * yp, :, zp * 128 : zp * 128 + 128] = jnp.concatenate(
                    [a[:, :64], b[:, :64]], axis=1
                )
                piece_out[fx * NY + 2 * yp + 1, :, zp * 128 : zp * 128 + 128] = jnp.concatenate(
                    [a[:, 64:], b[:, 64:]], axis=1
                )
    local(piece_out.at[f], pieces.at[f], rs.at[5])

    def plane_pieces(t, carry):
        p = (f + t) % PLANE
        send(piece_out.at[p], pieces.at[f], ss.at[5], rs.at[5], p // NY, z, p % NY, core)
        return carry

    lax.fori_loop(1, PLANE, plane_pieces, 0)
    lax.fori_loop(1, NZ * NC, line_w, 0)

    wait_bytes(kv.at[0], rs.at[1])
    for t in range(1, NY):
        send(kv.at[y], kv.at[y], ss.at[6], kv_rs.at[t - 1], x, z, (y + t) % NY, core)
    wait_bytes(queries.at[0], rs.at[2])
    for t in range(1, NX * NC):
        p = (xc + t) % (NX * NC)
        send(queries.at[xc], queries.at[xc], ss.at[7], rs.at[6], p // NC, z, y, p % NC)
    lax.fori_loop(1, NZ, line_cq, 0)

    wait_bytes(pieces, rs.at[5])
    piece = pieces[(owner // (NC * NY * NZ)) * NY + (owner // NC) % NY]
    for r in range(4):
        for c in range(2):
            sub_out[r * 2 + c] = piece[r * 16 : r * 16 + 16, c * 256 : c * 256 + 256]
    local(sub_out.at[z], subs.at[z], rs.at[7])

    def line_subs(t, carry):
        zz = (z + t) % NZ
        send(sub_out.at[zz], subs.at[z], ss.at[8], rs.at[7], x, zz, y, core)
        return carry

    lax.fori_loop(1, NZ, line_subs, 0)

    for t in range(1, NY):
        wait_bytes(kv.at[0], kv_rs.at[t - 1])
    wait_bytes(queries.at[pl.ds(0, 3)], rs.at[6])

    def self_part(s):
        keys = kv[:, 0].reshape(NY * SLOT, HEAD_DIM)
        values = kv[:, 1].reshape(NY * SLOT, HEAD_DIM)
        scores = dot_last(keys, queries[s]) * SCALE
        top = jnp.max(scores, axis=0, keepdims=True)
        weights = jnp.exp(scores - top)
        total = jnp.sum(weights, axis=0, keepdims=True)
        acc = dot_first(values, weights.astype(BF16)) / total
        return acc.astype(BF16), top, total

    def self_send(t):
        p = (xc + t) % (NX * NC)
        acc, top, total = self_part(p)
        acc_out[p] = acc
        stat_out[p, 0:1, :] = top
        stat_out[p, 1:2, :] = total
        send(acc_out.at[p], accs.at[xc], ss.at[9], acc_rs.at[t - 1], p // NC, z, y, p % NC)
        send(stat_out.at[p], stats.at[xc], ss.at[10], stat_rs.at[t - 1], p // NC, z, y, p % NC)

    self_send(1)

    wait_bytes(subs, rs.at[7])
    sub_mine[...] = subs[(owner // (NC * NY)) % NZ]
    my_sub = prompt.at[z % 2, rows((core * 4 + z // 2) * 16, 16), :]
    local(sub_mine, my_sub, rs.at[8])

    def line_prompt(t, carry):
        p = (z * NC + core + t) % (NZ * NC)
        send(sub_mine, my_sub, ss.at[11], rs.at[8], x, p // NC, y, p % NC)
        return carry

    lax.fori_loop(1, NZ * NC, line_prompt, 0)

    self_send(2)

    wait_bytes(weight, rs.at[4])
    wait_bytes(prompt, rs.at[8])
    part = jnp.dot(prompt[0], weight[0:256], preferred_element_type=F32)
    part = part + jnp.dot(prompt[1], weight[256:512], preferred_element_type=F32)
    part_out[...] = part.reshape(PLANE, 16, HEAD_DIM)
    local(part_out.at[f], parts.at[f], rs.at[9])

    def plane_parts(t, carry):
        p = (f + t) % PLANE
        send(part_out.at[p], parts.at[f], ss.at[12], rs.at[9], p // NY, z, p % NY, core)
        return carry

    lax.fori_loop(1, PLANE, plane_parts, 0)

    self_send(3)
    acc, top, total = self_part(xc)
    accs[xc] = acc
    stats[xc, 0:1, :] = top
    stats[xc, 1:2, :] = total

    wait_bytes(parts, rs.at[9])
    row_mine[...] = jnp.sum(parts[...], axis=0).astype(BF16)
    my_rows = cross_kv.at[core, rows(f * 16, 16), :]
    local(row_mine, my_rows, rs.at[10])

    def plane_rows(t, carry):
        p = (f * NC + core + t) % (PLANE * NC)
        pf = p // NC
        send(row_mine, my_rows, ss.at[13], rs.at[10], pf // NY, z, pf % NY, p % NC)
        return carry

    lax.fori_loop(1, PLANE * NC, plane_rows, 0)

    for t in range(1, NX * NC):
        wait_bytes(accs.at[0], acc_rs.at[t - 1])
        wait_bytes(stats.at[0], stat_rs.at[t - 1])
    tops = [stats[s, 0:1, :] for s in range(NX * NC)]
    top = jnp.maximum(jnp.maximum(tops[0], tops[1]), jnp.maximum(tops[2], tops[3]))
    shares = [stats[s, 1:2, :] * jnp.exp(tops[s] - top) for s in range(NX * NC)]
    whole = shares[0] + shares[1] + shares[2] + shares[3]
    mixed = jnp.zeros((HEAD_DIM, SLOT), F32)
    for s in range(NX * NC):
        mixed = mixed + accs[s].astype(F32) * (shares[s] / whole)

    wait_bytes(cross_q, rs.at[3])
    wait_bytes(cross_kv, rs.at[10])
    scores = dot_last(cross_kv[0], cross_q[...]) * SCALE
    valid = lax.broadcasted_iota(jnp.int32, scores.shape, 0) < len_ref[0]
    scores = jnp.where(valid, scores, -1e30)
    weights = jnp.exp(scores - jnp.max(scores, axis=0, keepdims=True))
    total = jnp.sum(weights, axis=0, keepdims=True)
    mixed = mixed + dot_first(cross_kv[1], weights.astype(BF16)) / total
    out_rows[...] = mixed.T.astype(BF16)

    local(out_rows.at[rows(z * TOK, TOK), :], out_ref.at[:, head_columns(z)], rs.at[11])

    def line_out(t, carry):
        zz = (z + t) % NZ
        send(out_rows.at[rows(zz * TOK, TOK), :], out_ref.at[:, head_columns(z)], ss.at[14], rs.at[11], x, zz, y, core)
        return carry

    lax.fori_loop(1, NZ, line_out, 0)

    wait_bytes(slots.at[0], ss.at[0])
    wait_bytes(kv.at[0, :, pl.ds(0, 224), :], ss.at[1])
    wait_bytes(queries.at[0, pl.ds(0, 224), :], ss.at[2])
    wait_bytes(queries.at[0, pl.ds(0, 224), :], ss.at[3])
    wait_bytes(weight.at[pl.ds(0, 480), :], ss.at[4])
    wait_bytes(pieces.at[pl.ds(0, 7)], ss.at[5])
    wait_bytes(kv.at[pl.ds(0, 3)], ss.at[6])
    wait_bytes(queries.at[pl.ds(0, 3)], ss.at[7])
    wait_bytes(subs.at[pl.ds(0, 7)], ss.at[8])
    wait_bytes(accs.at[pl.ds(0, 3)], ss.at[9])
    wait_bytes(stats.at[pl.ds(0, 3)], ss.at[10])
    wait_bytes(weight.at[pl.ds(0, 480), :], ss.at[11])
    wait_bytes(parts.at[pl.ds(0, 7)], ss.at[12])
    wait_bytes(cross_q.at[pl.ds(0, 240), :], ss.at[13])
    wait_bytes(cross_q.at[pl.ds(0, 224), :], ss.at[14])
    wait_bytes(out_ref, rs.at[11])


def on_device(queries, keys, values, cross_queries, text_states, cross_kv_weight, owner, prompt_len):
    smem = pl.BlockSpec(memory_space=pltpu.SMEM)
    hbm = pl.BlockSpec(memory_space=pltpu.HBM)
    return pl.pallas_call(
        kernel,
        out_shape=jax.ShapeDtypeStruct((TOK, HEADS * HEAD_DIM), BF16),
        in_specs=[smem, smem] + [hbm] * 6,
        out_specs=pl.BlockSpec(memory_space=pltpu.VMEM),
        scratch_shapes=[
            pltpu.VMEM((NC, 64, 4096), BF16),
            pltpu.VMEM((PLANE, 64, 512), BF16),
            pltpu.VMEM((PLANE, 64, 512), BF16),
            pltpu.VMEM((NZ, 16, 256), BF16),
            pltpu.VMEM((NZ, 16, 256), BF16),
            pltpu.VMEM((16, 256), BF16),
            pltpu.VMEM((2, 128, 256), BF16),
            pltpu.VMEM((512, HEAD_DIM), BF16),
            pltpu.VMEM((NY, 2, SLOT, HEAD_DIM), BF16),
            pltpu.VMEM((NX * NC, SLOT, HEAD_DIM), BF16),
            pltpu.VMEM((SLOT, HEAD_DIM), BF16),
            pltpu.VMEM((PLANE, 16, HEAD_DIM), F32),
            pltpu.VMEM((PLANE, 16, HEAD_DIM), F32),
            pltpu.VMEM((16, HEAD_DIM), BF16),
            pltpu.VMEM((2, 128, HEAD_DIM), BF16),
            pltpu.VMEM((NX * NC, HEAD_DIM, SLOT), BF16),
            pltpu.VMEM((NX * NC, HEAD_DIM, SLOT), BF16),
            pltpu.VMEM((NX * NC, 8, SLOT), F32),
            pltpu.VMEM((NX * NC, 8, SLOT), F32),
            pltpu.VMEM((SLOT, HEAD_DIM), BF16),
            pltpu.SemaphoreType.DMA((15,)),
            pltpu.SemaphoreType.DMA((12,)),
            pltpu.SemaphoreType.DMA((NY - 1,)),
            pltpu.SemaphoreType.DMA((NX * NC - 1,)),
            pltpu.SemaphoreType.DMA((NX * NC - 1,)),
        ],
        compiler_params=pltpu.CompilerParams(
            collective_id=0, has_side_effects=True, vmem_limit_bytes=56 * 1024 * 1024
        ),
        cost_estimate=pl.CostEstimate(flops=700_000_000, bytes_accessed=2_000_000, transcendentals=1_100_000),
    )(owner, prompt_len, queries, keys, values, cross_queries, text_states, cross_kv_weight)


def solution(mesh):
    return jax.shard_map(
        on_device,
        mesh=mesh,
        in_specs=(
            P(("batch", "seq"), None),
            P(("batch", "seq"), None),
            P(("batch", "seq"), None),
            P(("batch", "seq"), None),
            P(("batch", "seq"), None, None),
            P("seq", None),
            P("batch"),
            P("batch"),
        ),
        out_specs=P(("batch", "seq"), None),
        check_vma=False,
    )
```

```python
import math

import jax
import jax.numpy as jnp
from jax import lax
from jax.experimental import pallas as pl
from jax.experimental.pallas import tpu as pltpu
from jax.sharding import PartitionSpec as P

HEAD_DIM = 128
HEADS = 8
NX, NZ, NY, NC = 2, 8, 4, 2
PLANE = NX * NY
TOK = 32
SLOT = TOK * NZ
SCALE = math.log2(math.e) / math.sqrt(HEAD_DIM)
HALF = 64
F32 = jnp.float32
BF16 = jnp.bfloat16


def index_of(x, z, y, core):
    return ((x * NZ + z) * NY + y) * NC + core


def send(src, dst, send_sem, recv_sem, x, z, y, core):
    pltpu.make_async_remote_copy(
        src_ref=src,
        dst_ref=dst,
        send_sem=send_sem,
        recv_sem=recv_sem,
        device_id={"seq": index_of(x, z, y, core)},
        device_id_type=pl.DeviceIdType.MESH,
    ).start()


def local(src, dst, sem):
    pltpu.make_async_copy(src, dst, sem).start()


def wait_bytes(ref, sem):
    pltpu.make_async_copy(ref, ref, sem).wait()


def head_columns(head):
    return pl.ds(pl.multiple_of(head * HEAD_DIM, HEAD_DIM), HEAD_DIM)


def rows(start, count):
    return pl.ds(pl.multiple_of(start, count), count)


def dot_last(a, b):
    return lax.dot_general(a, b, (((1,), (1,)), ((), ())), preferred_element_type=F32)


def dot_first(a, b):
    return lax.dot_general(a, b, (((0,), (0,)), ((), ())), preferred_element_type=F32)


def kernel(
    owner_ref,
    len_ref,
    q_hbm,
    k_hbm,
    v_hbm,
    cq_hbm,
    text_hbm,
    w_hbm,
    out_ref,
    slots,
    piece_out,
    pieces,
    sub_out,
    subs,
    sub_mine,
    prompt,
    weight,
    kv,
    queries,
    cross_q,
    parts,
    cross_kv,
    mixed,
    acc_out,
    accs,
    stat_out,
    stats,
    out_rows,
    ss,
    rs,
    kv_rs,
    acc_rs,
    stat_rs,
):
    me = lax.axis_index("seq")
    core = me % NC
    y = (me // NC) % NY
    z = (me // (NC * NY)) % NZ
    x = me // (NC * NY * NZ)
    f = x * NY + y
    xc = x * NC + core
    other = 1 - core

    local(text_hbm.at[0, rows(core * 64, 64), :], slots.at[core], rs.at[0])
    local(k_hbm.at[:, head_columns(z)], kv.at[y, 0, rows(z * TOK, TOK), :], rs.at[1])
    local(v_hbm.at[:, head_columns(z)], kv.at[y, 1, rows(z * TOK, TOK), :], rs.at[1])
    local(q_hbm.at[:, head_columns(z)], queries.at[xc, rows(z * TOK, TOK), :], rs.at[2])
    local(cq_hbm.at[:, head_columns(z)], cross_q.at[rows(z * TOK, TOK), :], rs.at[3])
    for j in range(2):
        local(w_hbm.at[:, head_columns(j * HEADS + z)], weight.at[j, z, core], rs.at[4])

    barrier = pltpu.get_barrier_semaphore()

    def greet(x, z, y, core):
        pl.semaphore_signal(
            barrier, inc=1, device_id={"seq": index_of(x, z, y, core)}, device_id_type=pl.DeviceIdType.MESH
        )

    def greet_line(t, carry):
        greet(x, (z + t) % NZ, y, core)
        return carry

    def greet_plane(t, carry):
        p = (f + t) % PLANE
        greet(p // NY, z, p % NY, core)
        return carry

    greet(x, z, y, other)
    greet(1 - x, z, y, other)
    lax.fori_loop(1, NZ, greet_line, 0)
    lax.fori_loop(1, PLANE, greet_plane, 0)
    pl.semaphore_wait(barrier, 2 + NZ - 1 + PLANE - 1)

    send(text_hbm.at[0, rows(other * 64, 64), :], slots.at[core], ss.at[0], rs.at[0], x, z, y, other)

    def line_kv(t, carry):
        zz = (z + t) % NZ
        send(k_hbm.at[:, head_columns(zz)], kv.at[y, 0, rows(z * TOK, TOK), :], ss.at[1], rs.at[1], x, zz, y, core)
        send(v_hbm.at[:, head_columns(zz)], kv.at[y, 1, rows(z * TOK, TOK), :], ss.at[1], rs.at[1], x, zz, y, core)
        return carry

    def line_q(t, carry):
        zz = (z + t) % NZ
        send(q_hbm.at[:, head_columns(zz)], queries.at[xc, rows(z * TOK, TOK), :], ss.at[2], rs.at[2], x, zz, y, core)
        return carry

    def line_cq(t, carry):
        zz = (z + t) % NZ
        send(cq_hbm.at[:, head_columns(zz)], cross_q.at[rows(z * TOK, TOK), :], ss.at[3], rs.at[3], x, zz, y, core)
        return carry

    def line_w(t, carry):
        zz = (z + t) % NZ
        for j in range(2):
            send(w_hbm.at[:, head_columns(j * HEADS + zz)], weight.at[j, z, core], ss.at[4], rs.at[4], x, zz, y, core)
        return carry

    lax.fori_loop(1, NZ, line_kv, 0)
    lax.fori_loop(1, NZ, line_q, 0)

    owner = owner_ref[0]
    owner_core = owner % NC
    wait_bytes(slots, rs.at[0])

    def cut_pair(pair):
        fx, yp = pair // 2, pair % 2
        for zp in range(NZ // 2):
            base = pl.multiple_of(fx * (NZ * 256) + yp * 128 + zp * 512, 128)
            a = slots[owner_core, :, pl.ds(base, 128)]
            b = slots[owner_core, :, pl.ds(pl.multiple_of(base + 256, 128), 128)]
            piece_out[pair * 2, :, zp * 128 : zp * 128 + 128] = jnp.concatenate([a[:, :64], b[:, :64]], axis=1)
            piece_out[pair * 2 + 1, :, zp * 128 : zp * 128 + 128] = jnp.concatenate([a[:, 64:], b[:, 64:]], axis=1)

    def send_piece(p):
        send(piece_out.at[p], pieces.at[f], ss.at[5], rs.at[5], p // NY, z, p % NY, core)

    def plane_pair(t, carry):
        pair = (f // 2 + t) % (PLANE // 2)
        cut_pair(pair)
        send_piece(pair * 2 + f % 2)
        send_piece(pair * 2 + 1 - f % 2)
        return carry

    lax.fori_loop(1, PLANE // 2, plane_pair, 0)
    cut_pair(f // 2)
    send_piece(f + 1 - 2 * (f % 2))
    local(piece_out.at[f], pieces.at[f], rs.at[5])

    lax.fori_loop(1, NZ, line_w, 0)
    lax.fori_loop(1, NZ, line_cq, 0)

    wait_bytes(kv.at[0], rs.at[1])
    for t in (2, 1, 3):
        send(kv.at[y], kv.at[y], ss.at[6], kv_rs.at[t - 1], x, z, (y + t) % NY, core)
    wait_bytes(queries.at[0], rs.at[2])
    for t in (2, 1, 3):
        p = (xc + t) % (NX * NC)
        send(queries.at[xc], queries.at[xc], ss.at[7], rs.at[6], p // NC, z, y, p % NC)

    wait_bytes(pieces, rs.at[5])
    piece = pieces[(owner // (NC * NY * NZ)) * NY + (owner // NC) % NY]
    for r in range(4):
        for c in range(2):
            sub_out[r * 2 + c] = piece[r * 16 : r * 16 + 16, c * 256 : c * 256 + 256]
    local(sub_out.at[z], subs.at[z], rs.at[7])

    def line_subs(t, carry):
        zz = (z + t) % NZ
        send(sub_out.at[zz], subs.at[z], ss.at[8], rs.at[7], x, zz, y, core)
        return carry

    lax.fori_loop(1, NZ, line_subs, 0)

    wait_bytes(weight.at[:, :, 0], rs.at[4])
    send(weight.at[:, :, core], weight.at[:, :, core], ss.at[14], rs.at[9], x, z, y, other)

    wait_bytes(subs, rs.at[7])
    sub_mine[...] = subs[(owner // (NC * NY)) % NZ]
    my_sub = prompt.at[z % 2, rows((z // 2) * 16, 16), :]
    local(sub_mine, my_sub, rs.at[8])

    def line_prompt(t, carry):
        send(sub_mine, my_sub, ss.at[11], rs.at[8], x, (z + t) % NZ, y, core)
        return carry

    lax.fori_loop(1, NZ, line_prompt, 0)

    for t in range(1, NY):
        wait_bytes(kv.at[0], kv_rs.at[t - 1])
    wait_bytes(queries.at[pl.ds(0, 3)], rs.at[6])

    def self_part(s):
        keys = kv[:, 0].reshape(NY * SLOT, HEAD_DIM)
        values = kv[:, 1].reshape(NY * SLOT, HEAD_DIM)
        scores = dot_last(keys, queries[s])
        top = jnp.max(scores, axis=0, keepdims=True)
        weights = jnp.exp2((scores - top) * SCALE)
        total = jnp.sum(weights, axis=0, keepdims=True)
        acc = dot_first(values, weights.astype(BF16)) * (1.0 / total)
        return acc.astype(BF16), top, total

    for t in (2, 1, 3):
        p = (xc + t) % (NX * NC)
        acc, top, total = self_part(p)
        acc_out[p] = acc
        stat_out[p, 0:1, :] = top
        stat_out[p, 1:2, :] = total
        send(acc_out.at[p], accs.at[xc], ss.at[9], acc_rs.at[t - 1], p // NC, z, y, p % NC)
        send(stat_out.at[p], stats.at[xc], ss.at[10], stat_rs.at[t - 1], p // NC, z, y, p % NC)

    wait_bytes(weight.at[:, :, 0], rs.at[9])
    wait_bytes(prompt, rs.at[8])
    for j in range(2):
        columns = weight[j].reshape(512, HEAD_DIM)
        part = jnp.dot(prompt[0], columns[:256], preferred_element_type=F32)
        part = part + jnp.dot(prompt[1], columns[256:], preferred_element_type=F32)
        parts[f, j] = part.astype(BF16)

    def plane_parts(t, carry):
        p = (f + t) % PLANE
        send(parts.at[f], parts.at[f], ss.at[12], rs.at[10], p // NY, z, p % NY, core)
        return carry

    lax.fori_loop(1, PLANE, plane_parts, 0)

    acc, top, total = self_part(xc)
    accs[xc] = acc
    stats[xc, 0:1, :] = top
    stats[xc, 1:2, :] = total

    for t in range(1, NX * NC):
        wait_bytes(accs.at[0], acc_rs.at[t - 1])
        wait_bytes(stats.at[0], stat_rs.at[t - 1])
    tops = [stats[s, 0:1, :] for s in range(NX * NC)]
    top = jnp.maximum(jnp.maximum(tops[0], tops[1]), jnp.maximum(tops[2], tops[3]))
    shares = [stats[s, 1:2, :] * jnp.exp2((tops[s] - top) * SCALE) for s in range(NX * NC)]
    whole = 1.0 / (shares[0] + shares[1] + shares[2] + shares[3])
    mixed[...] = sum(accs[s].astype(F32) * (shares[s] * whole) for s in range(NX * NC))

    wait_bytes(parts.at[pl.ds(0, 7)], rs.at[10])
    cross_kv[core] = jnp.sum(parts[...].astype(F32), axis=0).astype(BF16)
    send(cross_kv.at[core], cross_kv.at[core], ss.at[13], rs.at[12], x, z, y, other)

    wait_bytes(cross_q, rs.at[3])
    wait_bytes(cross_kv.at[0], rs.at[12])
    cross_keys = cross_kv[:, 0].reshape(NC * HALF, HEAD_DIM)
    cross_values = cross_kv[:, 1].reshape(NC * HALF, HEAD_DIM)
    scores = dot_last(cross_keys, cross_q[...])
    valid = lax.broadcasted_iota(jnp.int32, scores.shape, 0) < len_ref[0]
    scores = jnp.where(valid, scores, -1e30)
    weights = jnp.exp2((scores - jnp.max(scores, axis=0, keepdims=True)) * SCALE)
    total = jnp.sum(weights, axis=0, keepdims=True)
    result = mixed[...] + dot_first(cross_values, weights.astype(BF16)) * (1.0 / total)
    out_rows[...] = result.T.astype(BF16)

    local(out_rows.at[rows(z * TOK, TOK), :], out_ref.at[:, head_columns(z)], rs.at[11])

    def line_out(t, carry):
        zz = (z + t) % NZ
        send(out_rows.at[rows(zz * TOK, TOK), :], out_ref.at[:, head_columns(z)], ss.at[15], rs.at[11], x, zz, y, core)
        return carry

    lax.fori_loop(1, NZ, line_out, 0)

    wait_bytes(slots.at[0], ss.at[0])
    wait_bytes(kv.at[0, :, pl.ds(0, 224), :], ss.at[1])
    wait_bytes(queries.at[0, pl.ds(0, 224), :], ss.at[2])
    wait_bytes(queries.at[0, pl.ds(0, 224), :], ss.at[3])
    wait_bytes(kv.at[0, :, pl.ds(0, 224), :], ss.at[4])
    wait_bytes(pieces.at[pl.ds(0, 7)], ss.at[5])
    wait_bytes(kv.at[pl.ds(0, 3)], ss.at[6])
    wait_bytes(queries.at[pl.ds(0, 3)], ss.at[7])
    wait_bytes(subs.at[pl.ds(0, 7)], ss.at[8])
    wait_bytes(accs.at[pl.ds(0, 3)], ss.at[9])
    wait_bytes(stats.at[pl.ds(0, 3)], ss.at[10])
    wait_bytes(subs.at[pl.ds(0, 7)], ss.at[11])
    wait_bytes(parts.at[pl.ds(0, 7)], ss.at[12])
    wait_bytes(cross_kv.at[0], ss.at[13])
    wait_bytes(weight.at[:, :, 0], ss.at[14])
    wait_bytes(cross_q.at[pl.ds(0, 224), :], ss.at[15])
    wait_bytes(out_ref, rs.at[11])


def on_device(queries, keys, values, cross_queries, text_states, cross_kv_weight, owner, prompt_len):
    smem = pl.BlockSpec(memory_space=pltpu.SMEM)
    hbm = pl.BlockSpec(memory_space=pltpu.HBM)
    return pl.pallas_call(
        kernel,
        out_shape=jax.ShapeDtypeStruct((TOK, HEADS * HEAD_DIM), BF16),
        in_specs=[smem, smem] + [hbm] * 6,
        out_specs=pl.BlockSpec(memory_space=pltpu.VMEM),
        scratch_shapes=[
            pltpu.VMEM((NC, 64, 4096), BF16),
            pltpu.VMEM((PLANE, 64, 512), BF16),
            pltpu.VMEM((PLANE, 64, 512), BF16),
            pltpu.VMEM((NZ, 16, 256), BF16),
            pltpu.VMEM((NZ, 16, 256), BF16),
            pltpu.VMEM((16, 256), BF16),
            pltpu.VMEM((2, HALF, 256), BF16),
            pltpu.VMEM((2, NZ, NC, TOK, HEAD_DIM), BF16),
            pltpu.VMEM((NY, 2, SLOT, HEAD_DIM), BF16),
            pltpu.VMEM((NX * NC, SLOT, HEAD_DIM), BF16),
            pltpu.VMEM((SLOT, HEAD_DIM), BF16),
            pltpu.VMEM((PLANE, 2, HALF, HEAD_DIM), BF16),
            pltpu.VMEM((NC, 2, HALF, HEAD_DIM), BF16),
            pltpu.VMEM((HEAD_DIM, SLOT), F32),
            pltpu.VMEM((NX * NC, HEAD_DIM, SLOT), BF16),
            pltpu.VMEM((NX * NC, HEAD_DIM, SLOT), BF16),
            pltpu.VMEM((NX * NC, 8, SLOT), F32),
            pltpu.VMEM((NX * NC, 8, SLOT), F32),
            pltpu.VMEM((SLOT, HEAD_DIM), BF16),
            pltpu.SemaphoreType.DMA((16,)),
            pltpu.SemaphoreType.DMA((13,)),
            pltpu.SemaphoreType.DMA((NY - 1,)),
            pltpu.SemaphoreType.DMA((NX * NC - 1,)),
            pltpu.SemaphoreType.DMA((NX * NC - 1,)),
        ],
        compiler_params=pltpu.CompilerParams(
            collective_id=0, has_side_effects=True, vmem_limit_bytes=56 * 1024 * 1024
        ),
        cost_estimate=pl.CostEstimate(flops=700_000_000, bytes_accessed=2_000_000, transcendentals=1_100_000),
    )(owner, prompt_len, queries, keys, values, cross_queries, text_states, cross_kv_weight)


def solution(mesh):
    return jax.shard_map(
        on_device,
        mesh=mesh,
        in_specs=(
            P(("batch", "seq"), None),
            P(("batch", "seq"), None),
            P(("batch", "seq"), None),
            P(("batch", "seq"), None),
            P(("batch", "seq"), None, None),
            P("seq", None),
            P("batch"),
            P("batch"),
        ),
        out_specs=P(("batch", "seq"), None),
        check_vma=False,
    )
```

```python
import math

import jax
import jax.numpy as jnp
from jax import lax
from jax.experimental import pallas as pl
from jax.experimental.pallas import tpu as pltpu
from jax.sharding import PartitionSpec as P

HEAD_DIM = 128
HEADS = 8
NX, NZ, NY, NC = 2, 8, 4, 2
PLANE = NX * NY
TOK = 32
SLOT = TOK * NZ
SCALE = math.log2(math.e) / math.sqrt(HEAD_DIM)
HALF = 64
LINE = (4, 3, 5, 2, 6, 1, 7)
ACROSS = (6, 5, 7, 2, 4, 1, 3)
F32 = jnp.float32
BF16 = jnp.bfloat16


def index_of(x, z, y, core):
    return ((x * NZ + z) * NY + y) * NC + core


def send(src, dst, send_sem, recv_sem, x, z, y, core):
    pltpu.make_async_remote_copy(
        src_ref=src,
        dst_ref=dst,
        send_sem=send_sem,
        recv_sem=recv_sem,
        device_id={"seq": index_of(x, z, y, core)},
        device_id_type=pl.DeviceIdType.MESH,
    ).start()


def each(steps, fn):
    for t in steps:
        fn(t)


def local(src, dst, sem):
    pltpu.make_async_copy(src, dst, sem).start()


def wait_bytes(ref, sem):
    pltpu.make_async_copy(ref, ref, sem).wait()


def head_columns(head):
    return pl.ds(pl.multiple_of(head * HEAD_DIM, HEAD_DIM), HEAD_DIM)


def rows(start, count):
    return pl.ds(pl.multiple_of(start, count), count)


def dot_last(a, b):
    return lax.dot_general(a, b, (((1,), (1,)), ((), ())), preferred_element_type=F32)


def dot_first(a, b):
    return lax.dot_general(a, b, (((0,), (0,)), ((), ())), preferred_element_type=F32)


def kernel(
    owner_ref,
    len_ref,
    q_hbm,
    k_hbm,
    v_hbm,
    cq_hbm,
    text_hbm,
    w_hbm,
    out_ref,
    slots,
    piece_out,
    pieces,
    sub_out,
    subs,
    sub_mine,
    prompt,
    weight,
    kv,
    queries,
    cross_q,
    part_out,
    parts,
    cross_kv,
    mixed,
    acc_out,
    accs,
    stat_out,
    stats,
    out_rows,
    ss,
    rs,
    kv_rs,
    acc_rs,
    stat_rs,
    vouch,
):
    me = lax.axis_index("seq")
    core = me % NC
    y = (me // NC) % NY
    z = (me // (NC * NY)) % NZ
    x = me // (NC * NY * NZ)
    f = x * NY + y
    xc = x * NC + core
    other = 1 - core

    local(text_hbm.at[0, rows(core * 64, 64), :], slots.at[core], rs.at[0])
    local(k_hbm.at[:, head_columns(z)], kv.at[y, 0, rows(z * TOK, TOK), :], rs.at[1])
    local(v_hbm.at[:, head_columns(z)], kv.at[y, 1, rows(z * TOK, TOK), :], rs.at[1])
    local(q_hbm.at[:, head_columns(z)], queries.at[xc, rows(z * TOK, TOK), :], rs.at[2])
    local(cq_hbm.at[:, head_columns(z)], cross_q.at[rows(z * TOK, TOK), :], rs.at[3])
    for j in range(2):
        local(w_hbm.at[:, head_columns(j * HEADS + z)], weight.at[j, z, core], rs.at[4])

    barrier = pltpu.get_barrier_semaphore()

    def greet(sem, x, z, y, core):
        pl.semaphore_signal(
            sem, inc=1, device_id={"seq": index_of(x, z, y, core)}, device_id_type=pl.DeviceIdType.MESH
        )

    for t in (2, 6):
        greet(barrier, x, (z + t) % NZ, y, core)
    for t in (2, 1, 3):
        greet(barrier, x, z, (y + t) % NY, core)
    for t in (1, 7):
        greet(barrier, x, (z + t) % NZ, y, core)
    greet(barrier, 1 - x, z, y, core)
    greet(barrier, x, z, y, other)
    pl.semaphore_wait(barrier, 9)

    send(text_hbm.at[0, rows(other * 64, 64), :], slots.at[core], ss.at[0], rs.at[0], x, z, y, other)

    greet(vouch.at[0], 1 - x, z, y, core)
    for t in (2, 6):
        greet(vouch.at[1], x, (z + t) % NZ, y, core)

    def line_kv(t):
        zz = (z + t) % NZ
        send(k_hbm.at[:, head_columns(zz)], kv.at[y, 0, rows(z * TOK, TOK), :], ss.at[1], rs.at[1], x, zz, y, core)
        send(v_hbm.at[:, head_columns(zz)], kv.at[y, 1, rows(z * TOK, TOK), :], ss.at[1], rs.at[1], x, zz, y, core)

    def line_q(t):
        zz = (z + t) % NZ
        send(q_hbm.at[:, head_columns(zz)], queries.at[xc, rows(z * TOK, TOK), :], ss.at[2], rs.at[2], x, zz, y, core)

    def line_cq(t):
        zz = (z + t) % NZ
        send(cq_hbm.at[:, head_columns(zz)], cross_q.at[rows(z * TOK, TOK), :], ss.at[3], rs.at[3], x, zz, y, core)

    def line_w(t):
        zz = (z + t) % NZ
        for j in range(2):
            send(w_hbm.at[:, head_columns(j * HEADS + zz)], weight.at[j, z, core], ss.at[4], rs.at[4], x, zz, y, core)

    each((2, 6, 1, 7), line_kv)
    pl.semaphore_wait(vouch.at[0], 1)
    pl.semaphore_wait(vouch.at[1], 2)
    each((4, 3, 5), line_kv)
    each(LINE, line_q)

    owner = owner_ref[0]
    owner_core = owner % NC
    wait_bytes(slots, rs.at[0])

    def cut_pair(pair):
        fx, yp = pair // 2, pair % 2
        for zp in range(NZ // 2):
            base = pl.multiple_of(fx * (NZ * 256) + yp * 128 + zp * 512, 128)
            a = slots[owner_core, :, pl.ds(base, 128)]
            b = slots[owner_core, :, pl.ds(pl.multiple_of(base + 256, 128), 128)]
            piece_out[pair * 2, :, zp * 128 : zp * 128 + 128] = jnp.concatenate([a[:, :64], b[:, :64]], axis=1)
            piece_out[pair * 2 + 1, :, zp * 128 : zp * 128 + 128] = jnp.concatenate([a[:, 64:], b[:, 64:]], axis=1)

    def send_piece(p):
        send(piece_out.at[p], pieces.at[f], ss.at[5], rs.at[5], p // NY, z, p % NY, core)

    def plane_pair(t, carry):
        pair = (f // 2 + t) % (PLANE // 2)
        cut_pair(pair)
        send_piece(pair * 2 + f % 2)
        send_piece(pair * 2 + 1 - f % 2)
        return carry

    lax.fori_loop(1, PLANE // 2, plane_pair, 0)
    cut_pair(f // 2)
    send_piece(f + 1 - 2 * (f % 2))
    local(piece_out.at[f], pieces.at[f], rs.at[5])

    each(LINE, line_w)
    each(LINE, line_cq)

    wait_bytes(kv.at[0], rs.at[1])
    for t in (2, 1, 3):
        send(kv.at[y], kv.at[y], ss.at[6], kv_rs.at[t - 1], x, z, (y + t) % NY, core)
    wait_bytes(queries.at[0], rs.at[2])
    for t in (2, 1, 3):
        p = (xc + t) % (NX * NC)
        send(queries.at[xc], queries.at[xc], ss.at[7], rs.at[6], p // NC, z, y, p % NC)

    wait_bytes(pieces, rs.at[5])
    piece = pieces[(owner // (NC * NY * NZ)) * NY + (owner // NC) % NY]
    for r in range(4):
        for c in range(2):
            sub_out[r * 2 + c] = piece[r * 16 : r * 16 + 16, c * 256 : c * 256 + 256]
    local(sub_out.at[z], subs.at[z], rs.at[7])

    def line_subs(t):
        zz = (z + t) % NZ
        send(sub_out.at[zz], subs.at[z], ss.at[8], rs.at[7], x, zz, y, core)

    each(LINE, line_subs)

    wait_bytes(weight.at[:, :, 0], rs.at[4])
    send(weight.at[:, :, core], weight.at[:, :, core], ss.at[14], rs.at[9], x, z, y, other)

    wait_bytes(subs, rs.at[7])
    sub_mine[...] = subs[(owner // (NC * NY)) % NZ]
    my_sub = prompt.at[z % 2, rows((z // 2) * 16, 16), :]
    local(sub_mine, my_sub, rs.at[8])

    def line_prompt(t):
        send(sub_mine, my_sub, ss.at[11], rs.at[8], x, (z + t) % NZ, y, core)

    each(LINE, line_prompt)

    for t in range(1, NY):
        wait_bytes(kv.at[0], kv_rs.at[t - 1])
    wait_bytes(queries.at[pl.ds(0, 3)], rs.at[6])

    def self_part(s):
        keys = kv[:, 0].reshape(NY * SLOT, HEAD_DIM)
        values = kv[:, 1].reshape(NY * SLOT, HEAD_DIM)
        scores = dot_last(keys, queries[s])
        top = jnp.max(scores, axis=0, keepdims=True)
        weights = jnp.exp2((scores - top) * SCALE)
        total = jnp.sum(weights, axis=0, keepdims=True)
        acc = dot_first(values, weights.astype(BF16)) * (1.0 / total)
        return acc.astype(BF16), top, total

    for t in (2, 1, 3):
        p = (xc + t) % (NX * NC)
        acc, top, total = self_part(p)
        acc_out[p] = acc
        stat_out[p, 0:1, :] = top
        stat_out[p, 1:2, :] = total
        send(acc_out.at[p], accs.at[xc], ss.at[9], acc_rs.at[t - 1], p // NC, z, y, p % NC)
        send(stat_out.at[p], stats.at[xc], ss.at[10], stat_rs.at[t - 1], p // NC, z, y, p % NC)

    wait_bytes(weight.at[:, :, 0], rs.at[9])
    wait_bytes(prompt, rs.at[8])
    for j in range(2):
        columns = weight[j].reshape(512, HEAD_DIM)
        part = jnp.dot(prompt[0], columns[:256], preferred_element_type=F32)
        part = part + jnp.dot(prompt[1], columns[256:], preferred_element_type=F32)
        part_out[:, j] = part.reshape(PLANE, 8, HEAD_DIM)

    def plane_parts(t):
        px, py = (x + t // NY) % NX, (y + t) % NY
        p = px * NY + py
        send(part_out.at[p], parts.at[f], ss.at[12], rs.at[10], px, z, py, core)

    each(ACROSS, plane_parts)
    parts[f] = part_out[f]

    acc, top, total = self_part(xc)
    accs[xc] = acc
    stats[xc, 0:1, :] = top
    stats[xc, 1:2, :] = total

    wait_bytes(parts.at[pl.ds(0, 7)], rs.at[10])
    cross_kv[core, f] = jnp.sum(parts[...], axis=0).reshape(16, HEAD_DIM).astype(BF16)

    def plane_rows(t):
        px, py = (x + t // NY) % NX, (y + t) % NY
        p = px * NY + py
        for c in (core, other):
            send(cross_kv.at[core, f], cross_kv.at[core, f], ss.at[13], rs.at[12], px, z, py, c)

    each(ACROSS, plane_rows)
    send(cross_kv.at[core, f], cross_kv.at[core, f], ss.at[13], rs.at[12], x, z, y, other)

    for t in range(1, NX * NC):
        wait_bytes(accs.at[0], acc_rs.at[t - 1])
        wait_bytes(stats.at[0], stat_rs.at[t - 1])
    tops = [stats[s, 0:1, :] for s in range(NX * NC)]
    top = jnp.maximum(jnp.maximum(tops[0], tops[1]), jnp.maximum(tops[2], tops[3]))
    shares = [stats[s, 1:2, :] * jnp.exp2((tops[s] - top) * SCALE) for s in range(NX * NC)]
    whole = 1.0 / (shares[0] + shares[1] + shares[2] + shares[3])
    mixed[...] = sum(accs[s].astype(F32) * (shares[s] * whole) for s in range(NX * NC))

    wait_bytes(cross_q, rs.at[3])
    wait_bytes(cross_q.at[pl.ds(0, 240), :], rs.at[12])
    cross = cross_kv[...].astype(F32)
    cross_keys = cross[:, :, :8].reshape(NC * HALF, HEAD_DIM).astype(BF16)
    cross_values = cross[:, :, 8:].reshape(NC * HALF, HEAD_DIM).astype(BF16)
    scores = dot_last(cross_keys, cross_q[...])
    valid = lax.broadcasted_iota(jnp.int32, scores.shape, 0) < len_ref[0]
    scores = jnp.where(valid, scores, -1e30)
    weights = jnp.exp2((scores - jnp.max(scores, axis=0, keepdims=True)) * SCALE)
    total = jnp.sum(weights, axis=0, keepdims=True)
    result = mixed[...] + dot_first(cross_values, weights.astype(BF16)) * (1.0 / total)
    out_rows[...] = result.T.astype(BF16)

    local(out_rows.at[rows(z * TOK, TOK), :], out_ref.at[:, head_columns(z)], rs.at[11])

    def line_out(t):
        zz = (z + t) % NZ
        send(out_rows.at[rows(zz * TOK, TOK), :], out_ref.at[:, head_columns(z)], ss.at[15], rs.at[11], x, zz, y, core)

    each(LINE, line_out)

    wait_bytes(slots.at[0], ss.at[0])
    wait_bytes(kv.at[0, :, pl.ds(0, 224), :], ss.at[1])
    wait_bytes(queries.at[0, pl.ds(0, 224), :], ss.at[2])
    wait_bytes(queries.at[0, pl.ds(0, 224), :], ss.at[3])
    wait_bytes(kv.at[0, :, pl.ds(0, 224), :], ss.at[4])
    wait_bytes(pieces.at[pl.ds(0, 7)], ss.at[5])
    wait_bytes(kv.at[pl.ds(0, 3)], ss.at[6])
    wait_bytes(queries.at[pl.ds(0, 3)], ss.at[7])
    wait_bytes(subs.at[pl.ds(0, 7)], ss.at[8])
    wait_bytes(accs.at[pl.ds(0, 3)], ss.at[9])
    wait_bytes(stats.at[pl.ds(0, 3)], ss.at[10])
    wait_bytes(subs.at[pl.ds(0, 7)], ss.at[11])
    wait_bytes(parts.at[pl.ds(0, 7)], ss.at[12])
    wait_bytes(cross_q.at[pl.ds(0, 240), :], ss.at[13])
    wait_bytes(weight.at[:, :, 0], ss.at[14])
    wait_bytes(cross_q.at[pl.ds(0, 224), :], ss.at[15])
    wait_bytes(out_ref, rs.at[11])


def on_device(queries, keys, values, cross_queries, text_states, cross_kv_weight, owner, prompt_len):
    smem = pl.BlockSpec(memory_space=pltpu.SMEM)
    hbm = pl.BlockSpec(memory_space=pltpu.HBM)
    return pl.pallas_call(
        kernel,
        out_shape=pltpu.VMEM((TOK, HEADS * HEAD_DIM), BF16),
        in_specs=[smem, smem] + [hbm] * 6,
        out_specs=pl.BlockSpec(memory_space=pltpu.VMEM),
        scratch_shapes=[
            pltpu.VMEM((NC, 64, 4096), BF16),
            pltpu.VMEM((PLANE, 64, 512), BF16),
            pltpu.VMEM((PLANE, 64, 512), BF16),
            pltpu.VMEM((NZ, 16, 256), BF16),
            pltpu.VMEM((NZ, 16, 256), BF16),
            pltpu.VMEM((16, 256), BF16),
            pltpu.VMEM((2, HALF, 256), BF16),
            pltpu.VMEM((2, NZ, NC, TOK, HEAD_DIM), BF16),
            pltpu.VMEM((NY, 2, SLOT, HEAD_DIM), BF16),
            pltpu.VMEM((NX * NC, SLOT, HEAD_DIM), BF16),
            pltpu.VMEM((SLOT, HEAD_DIM), BF16),
            pltpu.VMEM((PLANE, 2, 8, HEAD_DIM), F32),
            pltpu.VMEM((PLANE, 2, 8, HEAD_DIM), F32),
            pltpu.VMEM((NC, PLANE, 16, HEAD_DIM), BF16),
            pltpu.VMEM((HEAD_DIM, SLOT), F32),
            pltpu.VMEM((NX * NC, HEAD_DIM, SLOT), BF16),
            pltpu.VMEM((NX * NC, HEAD_DIM, SLOT), BF16),
            pltpu.VMEM((NX * NC, 8, SLOT), F32),
            pltpu.VMEM((NX * NC, 8, SLOT), F32),
            pltpu.VMEM((SLOT, HEAD_DIM), BF16),
            pltpu.SemaphoreType.DMA((16,)),
            pltpu.SemaphoreType.DMA((13,)),
            pltpu.SemaphoreType.DMA((NY - 1,)),
            pltpu.SemaphoreType.DMA((NX * NC - 1,)),
            pltpu.SemaphoreType.DMA((NX * NC - 1,)),
            pltpu.SemaphoreType.REGULAR((2,)),
        ],
        compiler_params=pltpu.CompilerParams(
            collective_id=0, has_side_effects=True, vmem_limit_bytes=56 * 1024 * 1024
        ),
        cost_estimate=pl.CostEstimate(flops=700_000_000, bytes_accessed=2_000_000, transcendentals=1_100_000),
    )(owner, prompt_len, queries, keys, values, cross_queries, text_states, cross_kv_weight)


def solution(mesh):
    return jax.shard_map(
        on_device,
        mesh=mesh,
        in_specs=(
            P(("batch", "seq"), None),
            P(("batch", "seq"), None),
            P(("batch", "seq"), None),
            P(("batch", "seq"), None),
            P(("batch", "seq"), None, None),
            P("seq", None),
            P("batch"),
            P("batch"),
        ),
        out_specs=P(("batch", "seq"), None),
        check_vma=False,
    )
```

```python
import math

import jax
import jax.numpy as jnp
from jax import lax
from jax.experimental import pallas as pl
from jax.experimental.pallas import tpu as pltpu
from jax.sharding import PartitionSpec as P

HEAD_DIM = 128
HEADS = 8
NX, NZ, NY, NC = 2, 8, 4, 2
PLANE = NX * NY
TOK = 32
SLOT = TOK * NZ
SCALE = math.log2(math.e) / math.sqrt(HEAD_DIM)
HALF = 64
LINE = (4, 3, 5, 2, 6, 1, 7)
ACROSS = (6, 5, 7, 2, 4, 1, 3)
F32 = jnp.float32
BF16 = jnp.bfloat16


def index_of(x, z, y, core):
    return ((x * NZ + z) * NY + y) * NC + core


def send(src, dst, send_sem, recv_sem, x, z, y, core):
    pltpu.make_async_remote_copy(
        src_ref=src,
        dst_ref=dst,
        send_sem=send_sem,
        recv_sem=recv_sem,
        device_id={"seq": index_of(x, z, y, core)},
        device_id_type=pl.DeviceIdType.MESH,
    ).start()


def each(steps, fn):
    for t in steps:
        fn(t)


def local(src, dst, sem):
    pltpu.make_async_copy(src, dst, sem).start()


def wait_bytes(ref, sem):
    pltpu.make_async_copy(ref, ref, sem).wait()


def head_columns(head):
    return pl.ds(pl.multiple_of(head * HEAD_DIM, HEAD_DIM), HEAD_DIM)


def half(x, i):
    return pl.ds(pl.multiple_of((x + 1 - i) % NX * 2048, 2048), 2048)


def rows(start, count):
    return pl.ds(pl.multiple_of(start, count), count)


def dot_last(a, b):
    return lax.dot_general(a, b, (((1,), (1,)), ((), ())), preferred_element_type=F32)


def dot_first(a, b):
    return lax.dot_general(a, b, (((0,), (0,)), ((), ())), preferred_element_type=F32)


def kernel(
    owner_ref,
    len_ref,
    q_hbm,
    k_hbm,
    v_hbm,
    cq_hbm,
    text_hbm,
    w_hbm,
    out_ref,
    slots_far,
    slots_near,
    piece_out,
    pieces,
    sub_out,
    subs,
    sub_mine,
    prompt,
    weight,
    kv,
    queries,
    cross_q,
    part_out,
    parts,
    cross_kv,
    mixed,
    acc_out,
    accs,
    stat_out,
    stats,
    out_rows,
    ss,
    rs,
    kv_rs,
    acc_rs,
    stat_rs,
    vouch,
    halves,
):
    me = lax.axis_index("seq")
    core = me % NC
    y = (me // NC) % NY
    z = (me // (NC * NY)) % NZ
    x = me // (NC * NY * NZ)
    f = x * NY + y
    xc = x * NC + core
    other = 1 - core
    halves_of = (slots_far, slots_near)

    barrier = pltpu.get_barrier_semaphore()

    def greet(sem, x, z, y, core):
        pl.semaphore_signal(
            sem, inc=1, device_id={"seq": index_of(x, z, y, core)}, device_id_type=pl.DeviceIdType.MESH
        )

    for t in (1, 7):
        greet(barrier, x, (z + t) % NZ, y, core)
    for t in (1, 3):
        greet(barrier, x, z, (y + t) % NY, core)
    greet(barrier, 1 - x, z, y, core)
    greet(barrier, x, z, y, other)
    for i in range(NX):
        local(text_hbm.at[0, rows(core * 64, 64), half(x, i)], halves_of[i].at[core], halves.at[i])
    pl.semaphore_wait(barrier, 6)

    theirs = rows(other * 64, 64)
    for i in range(NX):
        columns = half(x, i)
        send(text_hbm.at[0, theirs, columns], halves_of[i].at[core], ss.at[0], halves.at[i], x, z, y, other)

    def vouch_to(i, steps_y, steps_z):
        for t in steps_y:
            greet(vouch.at[i], x, z, (y + t) % NY, core)
        for t in steps_z:
            greet(vouch.at[i], x, (z + t) % NZ, y, core)

    vouch_to(0, (1, 3), ())
    vouch_to(1, (), (1, 7))

    local(k_hbm.at[:, head_columns(z)], kv.at[y, 0, rows(z * TOK, TOK), :], rs.at[1])
    local(v_hbm.at[:, head_columns(z)], kv.at[y, 1, rows(z * TOK, TOK), :], rs.at[1])
    local(q_hbm.at[:, head_columns(z)], queries.at[xc, rows(z * TOK, TOK), :], rs.at[2])
    local(cq_hbm.at[:, head_columns(z)], cross_q.at[rows(z * TOK, TOK), :], rs.at[3])
    for j in range(2):
        local(w_hbm.at[:, head_columns(j * HEADS + z)], weight.at[j, z, core], rs.at[4])

    def line_kv(t):
        zz = (z + t) % NZ
        send(k_hbm.at[:, head_columns(zz)], kv.at[y, 0, rows(z * TOK, TOK), :], ss.at[1], rs.at[1], x, zz, y, core)
        send(v_hbm.at[:, head_columns(zz)], kv.at[y, 1, rows(z * TOK, TOK), :], ss.at[1], rs.at[1], x, zz, y, core)

    def line_q(t):
        zz = (z + t) % NZ
        send(q_hbm.at[:, head_columns(zz)], queries.at[xc, rows(z * TOK, TOK), :], ss.at[2], rs.at[2], x, zz, y, core)

    def line_cq(t):
        zz = (z + t) % NZ
        send(cq_hbm.at[:, head_columns(zz)], cross_q.at[rows(z * TOK, TOK), :], ss.at[3], rs.at[3], x, zz, y, core)

    def line_w(t):
        zz = (z + t) % NZ
        for j in range(2):
            send(w_hbm.at[:, head_columns(j * HEADS + zz)], weight.at[j, z, core], ss.at[4], rs.at[4], x, zz, y, core)

    each((1, 7), line_kv)
    each((1, 7), line_q)
    pl.semaphore_wait(vouch.at[0], 2)
    greet(vouch.at[4], 1 - x, z, y, core)
    pl.semaphore_wait(vouch.at[1], 2)
    vouch_to(2, (), (1, 7))
    each((2, 6), line_kv)
    each((2, 6), line_q)

    owner = owner_ref[0]
    owner_core = owner % NC
    wait_bytes(slots_far, halves.at[0])

    def cut_pair(slots, pair):
        for zp in range(NZ // 2):
            base = pl.multiple_of(pair % 2 * 128 + zp * 512, 128)
            a = slots[owner_core, :, pl.ds(base, 128)]
            b = slots[owner_core, :, pl.ds(pl.multiple_of(base + 256, 128), 128)]
            piece_out[pair * 2, :, zp * 128 : zp * 128 + 128] = jnp.concatenate([a[:, :64], b[:, :64]], axis=1)
            piece_out[pair * 2 + 1, :, zp * 128 : zp * 128 + 128] = jnp.concatenate([a[:, 64:], b[:, 64:]], axis=1)

    def send_piece(p):
        send(piece_out.at[p], pieces.at[f], ss.at[5], rs.at[5], p // NY, z, p % NY, core)

    for i in range(NX):
        if i == 1:
            wait_bytes(slots_near, halves.at[1])
        px = (x + 1 - i) % NX
        for j in range(2):
            cut_pair(halves_of[i], px * 2 + j)
        for step in ((1, 3, 0), (2, 1, 3))[i]:
            send_piece(px * NY + (y + step) % NY)
    local(piece_out.at[f], pieces.at[f], rs.at[5])

    pl.semaphore_wait(vouch.at[2], 2)
    vouch_to(3, (), (1, 7))
    pl.semaphore_wait(vouch.at[4], 1)
    send_piece((1 - x) * NY + (y + 2) % NY)
    each((3, 5), line_kv)
    each((3, 5), line_q)
    pl.semaphore_wait(vouch.at[3], 2)
    each((4,), line_kv)
    each((4,), line_q)
    each(LINE, line_w)
    each(LINE, line_cq)

    wait_bytes(kv.at[0], rs.at[1])
    for t in (2, 1, 3):
        send(kv.at[y], kv.at[y], ss.at[6], kv_rs.at[t - 1], x, z, (y + t) % NY, core)
    wait_bytes(queries.at[0], rs.at[2])
    for t in (2, 1, 3):
        p = (xc + t) % (NX * NC)
        send(queries.at[xc], queries.at[xc], ss.at[7], rs.at[6], p // NC, z, y, p % NC)

    wait_bytes(pieces, rs.at[5])
    piece = pieces[(owner // (NC * NY * NZ)) * NY + (owner // NC) % NY]
    for r in range(4):
        for c in range(2):
            sub_out[r * 2 + c] = piece[r * 16 : r * 16 + 16, c * 256 : c * 256 + 256]

    def line_subs(t):
        zz = (z + t) % NZ
        send(sub_out.at[zz], subs.at[z], ss.at[8], rs.at[7], x, zz, y, core)

    each(LINE, line_subs)
    local(sub_out.at[z], subs.at[z], rs.at[7])

    wait_bytes(weight.at[:, :, 0], rs.at[4])
    send(weight.at[:, :, core], weight.at[:, :, core], ss.at[14], rs.at[9], x, z, y, other)

    wait_bytes(subs, rs.at[7])
    sub_mine[...] = subs[(owner // (NC * NY)) % NZ]
    my_sub = prompt.at[z % 2, rows((z // 2) * 16, 16), :]

    def line_prompt(t):
        send(sub_mine, my_sub, ss.at[11], rs.at[8], x, (z + t) % NZ, y, core)

    each(LINE, line_prompt)
    local(sub_mine, my_sub, rs.at[8])

    for t in range(1, NY):
        wait_bytes(kv.at[0], kv_rs.at[t - 1])
    wait_bytes(queries.at[pl.ds(0, 3)], rs.at[6])

    def self_part(s):
        keys = kv[:, 0].reshape(NY * SLOT, HEAD_DIM)
        values = kv[:, 1].reshape(NY * SLOT, HEAD_DIM)
        scores = dot_last(keys, queries[s])
        top = jnp.max(scores, axis=0, keepdims=True)
        weights = jnp.exp2((scores - top) * SCALE)
        total = jnp.sum(weights, axis=0, keepdims=True)
        acc = dot_first(values, weights.astype(BF16)) * (1.0 / total)
        return acc.astype(BF16), top, total

    for t in (2, 1, 3):
        p = (xc + t) % (NX * NC)
        acc, top, total = self_part(p)
        acc_out[p] = acc
        stat_out[p, 0:1, :] = top
        stat_out[p, 1:2, :] = total
        send(acc_out.at[p], accs.at[xc], ss.at[9], acc_rs.at[t - 1], p // NC, z, y, p % NC)
        send(stat_out.at[p], stats.at[xc], ss.at[10], stat_rs.at[t - 1], p // NC, z, y, p % NC)

    wait_bytes(weight.at[:, :, 0], rs.at[9])
    wait_bytes(prompt, rs.at[8])
    for j in range(2):
        columns = weight[j].reshape(512, HEAD_DIM)
        part = jnp.dot(prompt[0], columns[:256], preferred_element_type=F32)
        part = part + jnp.dot(prompt[1], columns[256:], preferred_element_type=F32)
        part_out[:, j] = part.reshape(PLANE, 8, HEAD_DIM)

    def plane_parts(t):
        px, py = (x + t // NY) % NX, (y + t) % NY
        p = px * NY + py
        send(part_out.at[p], parts.at[f], ss.at[12], rs.at[10], px, z, py, core)

    each(ACROSS, plane_parts)
    parts[f] = part_out[f]

    acc, top, total = self_part(xc)
    accs[xc] = acc
    stats[xc, 0:1, :] = top
    stats[xc, 1:2, :] = total

    wait_bytes(parts.at[pl.ds(0, 7)], rs.at[10])
    cross_kv[core, f] = jnp.sum(parts[...], axis=0).reshape(16, HEAD_DIM).astype(BF16)

    def plane_rows(t):
        px, py = (x + t // NY) % NX, (y + t) % NY
        p = px * NY + py
        for c in (core, other):
            send(cross_kv.at[core, f], cross_kv.at[core, f], ss.at[13], rs.at[12], px, z, py, c)

    each(ACROSS, plane_rows)
    send(cross_kv.at[core, f], cross_kv.at[core, f], ss.at[13], rs.at[12], x, z, y, other)

    for t in range(1, NX * NC):
        wait_bytes(accs.at[0], acc_rs.at[t - 1])
        wait_bytes(stats.at[0], stat_rs.at[t - 1])
    tops = [stats[s, 0:1, :] for s in range(NX * NC)]
    top = jnp.maximum(jnp.maximum(tops[0], tops[1]), jnp.maximum(tops[2], tops[3]))
    shares = [stats[s, 1:2, :] * jnp.exp2((tops[s] - top) * SCALE) for s in range(NX * NC)]
    whole = 1.0 / (shares[0] + shares[1] + shares[2] + shares[3])
    mixed[...] = sum(accs[s].astype(F32) * (shares[s] * whole) for s in range(NX * NC))

    wait_bytes(cross_q, rs.at[3])
    wait_bytes(cross_q.at[pl.ds(0, 240), :], rs.at[12])
    cross = cross_kv[...].astype(F32)
    cross_keys = cross[:, :, :8].reshape(NC * HALF, HEAD_DIM).astype(BF16)
    cross_values = cross[:, :, 8:].reshape(NC * HALF, HEAD_DIM).astype(BF16)
    scores = dot_last(cross_keys, cross_q[...])
    valid = lax.broadcasted_iota(jnp.int32, scores.shape, 0) < len_ref[0]
    scores = jnp.where(valid, scores, -1e30)
    weights = jnp.exp2((scores - jnp.max(scores, axis=0, keepdims=True)) * SCALE)
    total = jnp.sum(weights, axis=0, keepdims=True)
    result = mixed[...] + dot_first(cross_values, weights.astype(BF16)) * (1.0 / total)
    out_rows[...] = result.T.astype(BF16)


    def line_out(t):
        zz = (z + t) % NZ
        send(out_rows.at[rows(zz * TOK, TOK), :], out_ref.at[:, head_columns(z)], ss.at[15], rs.at[11], x, zz, y, core)

    each(LINE, line_out)
    local(out_rows.at[rows(z * TOK, TOK), :], out_ref.at[:, head_columns(z)], rs.at[11])

    wait_bytes(slots_far, ss.at[0])
    wait_bytes(kv.at[0, :, pl.ds(0, 224), :], ss.at[1])
    wait_bytes(queries.at[0, pl.ds(0, 224), :], ss.at[2])
    wait_bytes(queries.at[0, pl.ds(0, 224), :], ss.at[3])
    wait_bytes(kv.at[0, :, pl.ds(0, 224), :], ss.at[4])
    wait_bytes(pieces.at[pl.ds(0, 7)], ss.at[5])
    wait_bytes(kv.at[pl.ds(0, 3)], ss.at[6])
    wait_bytes(queries.at[pl.ds(0, 3)], ss.at[7])
    wait_bytes(subs.at[pl.ds(0, 7)], ss.at[8])
    wait_bytes(accs.at[pl.ds(0, 3)], ss.at[9])
    wait_bytes(stats.at[pl.ds(0, 3)], ss.at[10])
    wait_bytes(subs.at[pl.ds(0, 7)], ss.at[11])
    wait_bytes(parts.at[pl.ds(0, 7)], ss.at[12])
    wait_bytes(cross_q.at[pl.ds(0, 240), :], ss.at[13])
    wait_bytes(weight.at[:, :, 0], ss.at[14])
    wait_bytes(cross_q.at[pl.ds(0, 224), :], ss.at[15])
    wait_bytes(out_ref, rs.at[11])


def on_device(queries, keys, values, cross_queries, text_states, cross_kv_weight, owner, prompt_len):
    smem = pl.BlockSpec(memory_space=pltpu.SMEM)
    hbm = pl.BlockSpec(memory_space=pltpu.HBM)
    return pl.pallas_call(
        kernel,
        out_shape=pltpu.VMEM((TOK, HEADS * HEAD_DIM), BF16),
        in_specs=[smem, smem] + [hbm] * 6,
        out_specs=pl.BlockSpec(memory_space=pltpu.VMEM),
        scratch_shapes=[
            pltpu.VMEM((NC, 64, 2048), BF16),
            pltpu.VMEM((NC, 64, 2048), BF16),
            pltpu.VMEM((PLANE, 64, 512), BF16),
            pltpu.VMEM((PLANE, 64, 512), BF16),
            pltpu.VMEM((NZ, 16, 256), BF16),
            pltpu.VMEM((NZ, 16, 256), BF16),
            pltpu.VMEM((16, 256), BF16),
            pltpu.VMEM((2, HALF, 256), BF16),
            pltpu.VMEM((2, NZ, NC, TOK, HEAD_DIM), BF16),
            pltpu.VMEM((NY, 2, SLOT, HEAD_DIM), BF16),
            pltpu.VMEM((NX * NC, SLOT, HEAD_DIM), BF16),
            pltpu.VMEM((SLOT, HEAD_DIM), BF16),
            pltpu.VMEM((PLANE, 2, 8, HEAD_DIM), F32),
            pltpu.VMEM((PLANE, 2, 8, HEAD_DIM), F32),
            pltpu.VMEM((NC, PLANE, 16, HEAD_DIM), BF16),
            pltpu.VMEM((HEAD_DIM, SLOT), F32),
            pltpu.VMEM((NX * NC, HEAD_DIM, SLOT), BF16),
            pltpu.VMEM((NX * NC, HEAD_DIM, SLOT), BF16),
            pltpu.VMEM((NX * NC, 8, SLOT), F32),
            pltpu.VMEM((NX * NC, 8, SLOT), F32),
            pltpu.VMEM((SLOT, HEAD_DIM), BF16),
            pltpu.SemaphoreType.DMA((16,)),
            pltpu.SemaphoreType.DMA((13,)),
            pltpu.SemaphoreType.DMA((NY - 1,)),
            pltpu.SemaphoreType.DMA((NX * NC - 1,)),
            pltpu.SemaphoreType.DMA((NX * NC - 1,)),
            pltpu.SemaphoreType.REGULAR((5,)),
            pltpu.SemaphoreType.DMA((NX,)),
        ],
        compiler_params=pltpu.CompilerParams(
            collective_id=0, has_side_effects=True, vmem_limit_bytes=56 * 1024 * 1024
        ),
        cost_estimate=pl.CostEstimate(flops=700_000_000, bytes_accessed=2_000_000, transcendentals=1_100_000),
    )(owner, prompt_len, queries, keys, values, cross_queries, text_states, cross_kv_weight)


def solution(mesh):
    return jax.shard_map(
        on_device,
        mesh=mesh,
        in_specs=(
            P(("batch", "seq"), None),
            P(("batch", "seq"), None),
            P(("batch", "seq"), None),
            P(("batch", "seq"), None),
            P(("batch", "seq"), None, None),
            P("seq", None),
            P("batch"),
            P("batch"),
        ),
        out_specs=P(("batch", "seq"), None),
        check_vma=False,
    )
```

```python
import math

import jax
import jax.numpy as jnp
from jax import lax
from jax.experimental import pallas as pl
from jax.experimental.pallas import tpu as pltpu
from jax.sharding import PartitionSpec as P

HEAD_DIM = 128
HEADS = 8
NX, NZ, NY, NC = 2, 8, 4, 2
PLANE = NX * NY
TOK = 32
SLOT = TOK * NZ
SCALE = math.log2(math.e) / math.sqrt(HEAD_DIM)
HALF = 64
LINE = (4, 3, 5, 2, 6, 1, 7)
ACROSS = (6, 5, 7, 2, 4, 1, 3)
F32 = jnp.float32
BF16 = jnp.bfloat16


def index_of(x, z, y, core):
    return ((x * NZ + z) * NY + y) * NC + core


def send(src, dst, send_sem, recv_sem, x, z, y, core):
    pltpu.make_async_remote_copy(
        src_ref=src,
        dst_ref=dst,
        send_sem=send_sem,
        recv_sem=recv_sem,
        device_id={"seq": index_of(x, z, y, core)},
        device_id_type=pl.DeviceIdType.MESH,
    ).start()


def each(steps, fn):
    for t in steps:
        fn(t)


def local(src, dst, sem):
    pltpu.make_async_copy(src, dst, sem).start()


def wait_bytes(ref, sem):
    pltpu.make_async_copy(ref, ref, sem).wait()


def head_columns(head):
    return pl.ds(pl.multiple_of(head * HEAD_DIM, HEAD_DIM), HEAD_DIM)


def half(x, i):
    return pl.ds(pl.multiple_of((x + i) % NX * 2048, 2048), 2048)


def rows(start, count):
    return pl.ds(pl.multiple_of(start, count), count)


def dot_last(a, b):
    return lax.dot_general(a, b, (((1,), (1,)), ((), ())), preferred_element_type=F32)


def dot_first(a, b):
    return lax.dot_general(a, b, (((0,), (0,)), ((), ())), preferred_element_type=F32)


def kernel(
    owner_ref,
    len_ref,
    q_hbm,
    k_hbm,
    v_hbm,
    cq_hbm,
    text_hbm,
    w_hbm,
    out_ref,
    slots_a,
    slots_b,
    piece_out,
    pieces,
    sub_out,
    subs,
    sub_mine,
    prompt,
    weight,
    kv,
    queries,
    cross_q,
    part_out,
    parts,
    cross_kv,
    mixed,
    acc_out,
    accs,
    stat_out,
    stats,
    out_rows,
    ss,
    rs,
    kv_rs,
    acc_rs,
    stat_rs,
    vouch,
    halves,
):
    me = lax.axis_index("seq")
    core = me % NC
    y = (me // NC) % NY
    z = (me // (NC * NY)) % NZ
    x = me // (NC * NY * NZ)
    f = x * NY + y
    xc = x * NC + core
    other = 1 - core
    halves_of = (slots_a, slots_b)

    barrier = pltpu.get_barrier_semaphore()

    def greet(sem, x, z, y, core):
        pl.semaphore_signal(
            sem, inc=1, device_id={"seq": index_of(x, z, y, core)}, device_id_type=pl.DeviceIdType.MESH
        )

    for t in (2, 6, 1, 7):
        greet(barrier, x, (z + t) % NZ, y, 1)
    for t in (2, 1, 3):
        greet(barrier, x, z, (y + t) % NY, 1)
    greet(barrier, 1 - x, z, y, 1)
    greet(barrier, x, z, y, other)
    for i in range(NX):
        local(text_hbm.at[0, rows(core * 64, 64), half(x, i)], halves_of[i].at[core], halves.at[i])

    @pl.when(core == 0)
    def _():
        pl.semaphore_wait(barrier, 1)

    @pl.when(core == 1)
    def _():
        pl.semaphore_wait(barrier, 17)

    theirs = rows(other * 64, 64)
    for i in range(NX):
        columns = half(x, i)
        send(text_hbm.at[0, theirs, columns], halves_of[i].at[core], ss.at[0], halves.at[i], x, z, y, other)

    @pl.when(core == 1)
    def _():
        greet(vouch.at[0], x, z, y, 0)
        greet(vouch.at[1], 1 - x, z, y, 1)
        for t in (2, 6):
            greet(vouch.at[2], x, (z + t) % NZ, y, 1)

    local(k_hbm.at[:, head_columns(z)], kv.at[y, 0, rows(z * TOK, TOK), :], rs.at[1])
    local(v_hbm.at[:, head_columns(z)], kv.at[y, 1, rows(z * TOK, TOK), :], rs.at[1])
    local(q_hbm.at[:, head_columns(z)], queries.at[xc, rows(z * TOK, TOK), :], rs.at[2])
    local(cq_hbm.at[:, head_columns(z)], cross_q.at[rows(z * TOK, TOK), :], rs.at[3])
    for j in range(2):
        local(w_hbm.at[:, head_columns(j * HEADS + z)], weight.at[j, z, core], rs.at[4])

    def line_kv(t):
        zz = (z + t) % NZ
        send(k_hbm.at[:, head_columns(zz)], kv.at[y, 0, rows(z * TOK, TOK), :], ss.at[1], rs.at[1], x, zz, y, core)
        send(v_hbm.at[:, head_columns(zz)], kv.at[y, 1, rows(z * TOK, TOK), :], ss.at[1], rs.at[1], x, zz, y, core)

    def line_q(t):
        zz = (z + t) % NZ
        send(q_hbm.at[:, head_columns(zz)], queries.at[xc, rows(z * TOK, TOK), :], ss.at[2], rs.at[2], x, zz, y, core)

    def line_cq(t):
        zz = (z + t) % NZ
        send(cq_hbm.at[:, head_columns(zz)], cross_q.at[rows(z * TOK, TOK), :], ss.at[3], rs.at[3], x, zz, y, core)

    def line_w(t):
        zz = (z + t) % NZ
        for j in range(2):
            send(w_hbm.at[:, head_columns(j * HEADS + zz)], weight.at[j, z, core], ss.at[4], rs.at[4], x, zz, y, core)

    @pl.when(core == 0)
    def _():
        pl.semaphore_wait(vouch.at[0], 1)

    owner = owner_ref[0]
    owner_core = owner % NC
    wait_bytes(slots_a, halves.at[0])

    def cut_pair(slots, pair):
        for zp in range(NZ // 2):
            base = pl.multiple_of(pair % 2 * 128 + zp * 512, 128)
            a = slots[owner_core, :, pl.ds(base, 128)]
            b = slots[owner_core, :, pl.ds(pl.multiple_of(base + 256, 128), 128)]
            piece_out[pair * 2, :, zp * 128 : zp * 128 + 128] = jnp.concatenate([a[:, :64], b[:, :64]], axis=1)
            piece_out[pair * 2 + 1, :, zp * 128 : zp * 128 + 128] = jnp.concatenate([a[:, 64:], b[:, 64:]], axis=1)

    def send_piece(p):
        send(piece_out.at[p], pieces.at[f], ss.at[5], rs.at[5], p // NY, z, p % NY, core)

    for i in range(NX):
        if i == 1:
            wait_bytes(slots_b, halves.at[1])
        px = (x + i) % NX
        for j in range(2):
            cut_pair(halves_of[i], px * 2 + j)
        for step in ((2, 1, 3), (0,))[i]:
            send_piece(px * NY + (y + step) % NY)
    local(piece_out.at[f], pieces.at[f], rs.at[5])

    each((2, 6, 1, 7), line_kv)

    @pl.when(core == 1)
    def _():
        pl.semaphore_wait(vouch.at[1], 1)
        greet(vouch.at[3], x, z, y, 0)

    @pl.when(core == 0)
    def _():
        pl.semaphore_wait(vouch.at[3], 1)

    for step in (2, 1, 3):
        send_piece((1 - x) * NY + (y + step) % NY)

    @pl.when(core == 1)
    def _():
        pl.semaphore_wait(vouch.at[2], 2)
        greet(vouch.at[4], x, z, y, 0)

    @pl.when(core == 0)
    def _():
        pl.semaphore_wait(vouch.at[4], 1)

    each((4, 3, 5), line_kv)
    each(LINE, line_q)
    each(LINE, line_w)
    each(LINE, line_cq)

    wait_bytes(kv.at[0], rs.at[1])
    for t in (2, 1, 3):
        send(kv.at[y], kv.at[y], ss.at[6], kv_rs.at[t - 1], x, z, (y + t) % NY, core)
    wait_bytes(queries.at[0], rs.at[2])
    for t in (2, 1, 3):
        p = (xc + t) % (NX * NC)
        send(queries.at[xc], queries.at[xc], ss.at[7], rs.at[6], p // NC, z, y, p % NC)

    wait_bytes(pieces, rs.at[5])
    piece = pieces[(owner // (NC * NY * NZ)) * NY + (owner // NC) % NY]
    for r in range(4):
        for c in range(2):
            sub_out[r * 2 + c] = piece[r * 16 : r * 16 + 16, c * 256 : c * 256 + 256]

    def line_subs(t):
        zz = (z + t) % NZ
        send(sub_out.at[zz], subs.at[z], ss.at[8], rs.at[7], x, zz, y, core)

    each(LINE, line_subs)
    local(sub_out.at[z], subs.at[z], rs.at[7])

    wait_bytes(weight.at[:, :, 0], rs.at[4])
    send(weight.at[:, :, core], weight.at[:, :, core], ss.at[14], rs.at[9], x, z, y, other)

    wait_bytes(subs, rs.at[7])
    sub_mine[...] = subs[(owner // (NC * NY)) % NZ]
    my_sub = prompt.at[z % 2, rows((z // 2) * 16, 16), :]

    def line_prompt(t):
        send(sub_mine, my_sub, ss.at[11], rs.at[8], x, (z + t) % NZ, y, core)

    each(LINE, line_prompt)
    local(sub_mine, my_sub, rs.at[8])

    for t in range(1, NY):
        wait_bytes(kv.at[0], kv_rs.at[t - 1])
    wait_bytes(queries.at[pl.ds(0, 3)], rs.at[6])

    def self_part(s):
        keys = kv[:, 0].reshape(NY * SLOT, HEAD_DIM)
        values = kv[:, 1].reshape(NY * SLOT, HEAD_DIM)
        scores = dot_last(keys, queries[s])
        top = jnp.max(scores, axis=0, keepdims=True)
        weights = jnp.exp2((scores - top) * SCALE)
        total = jnp.sum(weights, axis=0, keepdims=True)
        acc = dot_first(values, weights.astype(BF16)) * (1.0 / total)
        return acc.astype(BF16), top, total

    for t in (2, 1, 3):
        p = (xc + t) % (NX * NC)
        acc, top, total = self_part(p)
        acc_out[p] = acc
        stat_out[p, 0:1, :] = top
        stat_out[p, 1:2, :] = total
        send(acc_out.at[p], accs.at[xc], ss.at[9], acc_rs.at[t - 1], p // NC, z, y, p % NC)
        send(stat_out.at[p], stats.at[xc], ss.at[10], stat_rs.at[t - 1], p // NC, z, y, p % NC)

    wait_bytes(weight.at[:, :, 0], rs.at[9])
    wait_bytes(prompt, rs.at[8])
    for j in range(2):
        columns = weight[j].reshape(512, HEAD_DIM)
        part = jnp.dot(prompt[0], columns[:256], preferred_element_type=F32)
        part = part + jnp.dot(prompt[1], columns[256:], preferred_element_type=F32)
        part_out[:, j] = part.reshape(PLANE, 8, HEAD_DIM)

    def plane_parts(t):
        px, py = (x + t // NY) % NX, (y + t) % NY
        p = px * NY + py
        send(part_out.at[p], parts.at[f], ss.at[12], rs.at[10], px, z, py, core)

    each(ACROSS, plane_parts)
    parts[f] = part_out[f]

    acc, top, total = self_part(xc)
    accs[xc] = acc
    stats[xc, 0:1, :] = top
    stats[xc, 1:2, :] = total

    wait_bytes(parts.at[pl.ds(0, 7)], rs.at[10])
    cross_kv[core, f] = jnp.sum(parts[...], axis=0).reshape(16, HEAD_DIM).astype(BF16)

    def plane_rows(t):
        px, py = (x + t // NY) % NX, (y + t) % NY
        p = px * NY + py
        for c in (core, other):
            send(cross_kv.at[core, f], cross_kv.at[core, f], ss.at[13], rs.at[12], px, z, py, c)

    each(ACROSS, plane_rows)
    send(cross_kv.at[core, f], cross_kv.at[core, f], ss.at[13], rs.at[12], x, z, y, other)

    for t in range(1, NX * NC):
        wait_bytes(accs.at[0], acc_rs.at[t - 1])
        wait_bytes(stats.at[0], stat_rs.at[t - 1])
    tops = [stats[s, 0:1, :] for s in range(NX * NC)]
    top = jnp.maximum(jnp.maximum(tops[0], tops[1]), jnp.maximum(tops[2], tops[3]))
    shares = [stats[s, 1:2, :] * jnp.exp2((tops[s] - top) * SCALE) for s in range(NX * NC)]
    whole = 1.0 / (shares[0] + shares[1] + shares[2] + shares[3])
    mixed[...] = sum(accs[s].astype(F32) * (shares[s] * whole) for s in range(NX * NC))

    wait_bytes(cross_q, rs.at[3])
    wait_bytes(cross_q.at[pl.ds(0, 240), :], rs.at[12])
    cross = cross_kv[...].astype(F32)
    cross_keys = cross[:, :, :8].reshape(NC * HALF, HEAD_DIM).astype(BF16)
    cross_values = cross[:, :, 8:].reshape(NC * HALF, HEAD_DIM).astype(BF16)
    scores = dot_last(cross_keys, cross_q[...])
    valid = lax.broadcasted_iota(jnp.int32, scores.shape, 0) < len_ref[0]
    scores = jnp.where(valid, scores, -1e30)
    weights = jnp.exp2((scores - jnp.max(scores, axis=0, keepdims=True)) * SCALE)
    total = jnp.sum(weights, axis=0, keepdims=True)
    result = mixed[...] + dot_first(cross_values, weights.astype(BF16)) * (1.0 / total)
    out_rows[...] = result.T.astype(BF16)


    def line_out(t):
        zz = (z + t) % NZ
        send(out_rows.at[rows(zz * TOK, TOK), :], out_ref.at[:, head_columns(z)], ss.at[15], rs.at[11], x, zz, y, core)

    each(LINE, line_out)
    local(out_rows.at[rows(z * TOK, TOK), :], out_ref.at[:, head_columns(z)], rs.at[11])

    wait_bytes(slots_a, ss.at[0])
    wait_bytes(kv.at[0, :, pl.ds(0, 224), :], ss.at[1])
    wait_bytes(queries.at[0, pl.ds(0, 224), :], ss.at[2])
    wait_bytes(queries.at[0, pl.ds(0, 224), :], ss.at[3])
    wait_bytes(kv.at[0, :, pl.ds(0, 224), :], ss.at[4])
    wait_bytes(pieces.at[pl.ds(0, 7)], ss.at[5])
    wait_bytes(kv.at[pl.ds(0, 3)], ss.at[6])
    wait_bytes(queries.at[pl.ds(0, 3)], ss.at[7])
    wait_bytes(subs.at[pl.ds(0, 7)], ss.at[8])
    wait_bytes(accs.at[pl.ds(0, 3)], ss.at[9])
    wait_bytes(stats.at[pl.ds(0, 3)], ss.at[10])
    wait_bytes(subs.at[pl.ds(0, 7)], ss.at[11])
    wait_bytes(parts.at[pl.ds(0, 7)], ss.at[12])
    wait_bytes(cross_q.at[pl.ds(0, 240), :], ss.at[13])
    wait_bytes(weight.at[:, :, 0], ss.at[14])
    wait_bytes(cross_q.at[pl.ds(0, 224), :], ss.at[15])
    wait_bytes(out_ref, rs.at[11])


def on_device(queries, keys, values, cross_queries, text_states, cross_kv_weight, owner, prompt_len):
    smem = pl.BlockSpec(memory_space=pltpu.SMEM)
    hbm = pl.BlockSpec(memory_space=pltpu.HBM)
    return pl.pallas_call(
        kernel,
        out_shape=pltpu.VMEM((TOK, HEADS * HEAD_DIM), BF16),
        in_specs=[smem, smem] + [hbm] * 6,
        out_specs=pl.BlockSpec(memory_space=pltpu.VMEM),
        scratch_shapes=[
            pltpu.VMEM((NC, 64, 2048), BF16),
            pltpu.VMEM((NC, 64, 2048), BF16),
            pltpu.VMEM((PLANE, 64, 512), BF16),
            pltpu.VMEM((PLANE, 64, 512), BF16),
            pltpu.VMEM((NZ, 16, 256), BF16),
            pltpu.VMEM((NZ, 16, 256), BF16),
            pltpu.VMEM((16, 256), BF16),
            pltpu.VMEM((2, HALF, 256), BF16),
            pltpu.VMEM((2, NZ, NC, TOK, HEAD_DIM), BF16),
            pltpu.VMEM((NY, 2, SLOT, HEAD_DIM), BF16),
            pltpu.VMEM((NX * NC, SLOT, HEAD_DIM), BF16),
            pltpu.VMEM((SLOT, HEAD_DIM), BF16),
            pltpu.VMEM((PLANE, 2, 8, HEAD_DIM), F32),
            pltpu.VMEM((PLANE, 2, 8, HEAD_DIM), F32),
            pltpu.VMEM((NC, PLANE, 16, HEAD_DIM), BF16),
            pltpu.VMEM((HEAD_DIM, SLOT), F32),
            pltpu.VMEM((NX * NC, HEAD_DIM, SLOT), BF16),
            pltpu.VMEM((NX * NC, HEAD_DIM, SLOT), BF16),
            pltpu.VMEM((NX * NC, 8, SLOT), F32),
            pltpu.VMEM((NX * NC, 8, SLOT), F32),
            pltpu.VMEM((SLOT, HEAD_DIM), BF16),
            pltpu.SemaphoreType.DMA((16,)),
            pltpu.SemaphoreType.DMA((13,)),
            pltpu.SemaphoreType.DMA((NY - 1,)),
            pltpu.SemaphoreType.DMA((NX * NC - 1,)),
            pltpu.SemaphoreType.DMA((NX * NC - 1,)),
            pltpu.SemaphoreType.REGULAR((5,)),
            pltpu.SemaphoreType.DMA((NX,)),
        ],
        compiler_params=pltpu.CompilerParams(
            collective_id=0, has_side_effects=True, vmem_limit_bytes=56 * 1024 * 1024
        ),
        cost_estimate=pl.CostEstimate(flops=700_000_000, bytes_accessed=2_000_000, transcendentals=1_100_000),
    )(owner, prompt_len, queries, keys, values, cross_queries, text_states, cross_kv_weight)


def solution(mesh):
    return jax.shard_map(
        on_device,
        mesh=mesh,
        in_specs=(
            P(("batch", "seq"), None),
            P(("batch", "seq"), None),
            P(("batch", "seq"), None),
            P(("batch", "seq"), None),
            P(("batch", "seq"), None, None),
            P("seq", None),
            P("batch"),
            P("batch"),
        ),
        out_specs=P(("batch", "seq"), None),
        check_vma=False,
    )
```

```python
import math

import jax
import jax.numpy as jnp
from jax import lax
from jax.experimental import pallas as pl
from jax.experimental.pallas import tpu as pltpu
from jax.sharding import PartitionSpec as P

HEAD_DIM = 128
HEADS = 8
NX, NZ, NY, NC = 2, 8, 4, 2
PLANE = NX * NY
TOK = 32
SLOT = TOK * NZ
SCALE = math.log2(math.e) / math.sqrt(HEAD_DIM)
HALF = 64
LINE = (4, 3, 5, 2, 6, 1, 7)
ACROSS = (6, 5, 7, 2, 4, 1, 3)
F32 = jnp.float32
BF16 = jnp.bfloat16


def index_of(x, z, y, core):
    return ((x * NZ + z) * NY + y) * NC + core


def send(src, dst, send_sem, recv_sem, x, z, y, core):
    pltpu.make_async_remote_copy(
        src_ref=src,
        dst_ref=dst,
        send_sem=send_sem,
        recv_sem=recv_sem,
        device_id={"seq": index_of(x, z, y, core)},
        device_id_type=pl.DeviceIdType.MESH,
    ).start()


def each(steps, fn):
    for t in steps:
        fn(t)


def local(src, dst, sem):
    pltpu.make_async_copy(src, dst, sem).start()


def wait_bytes(ref, sem):
    pltpu.make_async_copy(ref, ref, sem).wait()


def head_columns(head):
    return pl.ds(pl.multiple_of(head * HEAD_DIM, HEAD_DIM), HEAD_DIM)


def half(x, i):
    return pl.ds(pl.multiple_of((x + i) % NX * 2048, 2048), 2048)


def rows(start, count):
    return pl.ds(pl.multiple_of(start, count), count)


def dot_last(a, b):
    return lax.dot_general(a, b, (((1,), (1,)), ((), ())), preferred_element_type=F32)


def dot_first(a, b):
    return lax.dot_general(a, b, (((0,), (0,)), ((), ())), preferred_element_type=F32)


def kernel(
    owner_ref,
    len_ref,
    q_hbm,
    k_hbm,
    v_hbm,
    cq_hbm,
    text_hbm,
    w_hbm,
    out_ref,
    slots_a,
    slots_b,
    piece_out,
    pieces,
    sub_out,
    subs,
    sub_mine,
    prompt,
    weight,
    kv,
    queries,
    cross_q,
    part_out,
    parts,
    cross_kv,
    mixed,
    acc_out,
    accs,
    stat_out,
    stats,
    out_rows,
    ss,
    rs,
    kv_rs,
    acc_rs,
    stat_rs,
    vouch,
    halves,
):
    me = lax.axis_index("seq")
    core = me % NC
    y = (me // NC) % NY
    z = (me // (NC * NY)) % NZ
    x = me // (NC * NY * NZ)
    f = x * NY + y
    xc = x * NC + core
    other = 1 - core
    halves_of = (slots_a, slots_b)

    barrier = pltpu.get_barrier_semaphore()

    def greet(sem, x, z, y, core):
        pl.semaphore_signal(
            sem, inc=1, device_id={"seq": index_of(x, z, y, core)}, device_id_type=pl.DeviceIdType.MESH
        )

    for t in (2, 6, 1, 7):
        greet(barrier, x, (z + t) % NZ, y, 1)
    for t in (2, 1, 3):
        greet(barrier, x, z, (y + t) % NY, 1)
    greet(barrier, 1 - x, z, y, 1)
    greet(barrier, x, z, y, other)
    for i in range(NX):
        local(text_hbm.at[0, rows(core * 64, 64), half(x, i)], halves_of[i].at[core], halves.at[i])

    @pl.when(core == 0)
    def _():
        pl.semaphore_wait(barrier, 1)

    @pl.when(core == 1)
    def _():
        pl.semaphore_wait(barrier, 17)

    theirs = rows(other * 64, 64)
    for i in range(NX):
        columns = half(x, i)
        send(text_hbm.at[0, theirs, columns], halves_of[i].at[core], ss.at[0], halves.at[i], x, z, y, other)

    @pl.when(core == 1)
    def _():
        greet(vouch.at[0], x, z, y, 0)
        greet(vouch.at[1], 1 - x, z, y, 1)
        for t in (2, 6):
            greet(vouch.at[2], x, (z + t) % NZ, y, 1)

    local(k_hbm.at[:, head_columns(z)], kv.at[y, 0, rows(z * TOK, TOK), :], rs.at[1])
    local(v_hbm.at[:, head_columns(z)], kv.at[y, 1, rows(z * TOK, TOK), :], rs.at[1])
    local(q_hbm.at[:, head_columns(z)], queries.at[xc, rows(z * TOK, TOK), :], rs.at[2])
    local(cq_hbm.at[:, head_columns(z)], cross_q.at[rows(z * TOK, TOK), :], rs.at[3])
    for j in range(2):
        local(w_hbm.at[:, head_columns(j * HEADS + z)], weight.at[j, z, core], rs.at[4])

    def line_kv(t):
        zz = (z + t) % NZ
        send(k_hbm.at[:, head_columns(zz)], kv.at[y, 0, rows(z * TOK, TOK), :], ss.at[1], rs.at[1], x, zz, y, core)
        send(v_hbm.at[:, head_columns(zz)], kv.at[y, 1, rows(z * TOK, TOK), :], ss.at[1], rs.at[1], x, zz, y, core)

    def line_q(t):
        zz = (z + t) % NZ
        send(q_hbm.at[:, head_columns(zz)], queries.at[xc, rows(z * TOK, TOK), :], ss.at[2], rs.at[2], x, zz, y, core)

    def line_cq(t):
        zz = (z + t) % NZ
        send(cq_hbm.at[:, head_columns(zz)], cross_q.at[rows(z * TOK, TOK), :], ss.at[3], rs.at[3], x, zz, y, core)

    def line_w(t):
        zz = (z + t) % NZ
        for j in range(2):
            send(w_hbm.at[:, head_columns(j * HEADS + zz)], weight.at[j, z, core], ss.at[4], rs.at[4], x, zz, y, core)

    @pl.when(core == 0)
    def _():
        pl.semaphore_wait(vouch.at[0], 1)

    owner = owner_ref[0]
    owner_core = owner % NC
    wait_bytes(slots_a, halves.at[0])

    def cut_pair(slots, pair):
        for zp in range(NZ // 2):
            base = pl.multiple_of(pair % 2 * 128 + zp * 512, 128)
            a = slots[owner_core, :, pl.ds(base, 128)]
            b = slots[owner_core, :, pl.ds(pl.multiple_of(base + 256, 128), 128)]
            piece_out[pair * 2, :, zp * 128 : zp * 128 + 128] = jnp.concatenate([a[:, :64], b[:, :64]], axis=1)
            piece_out[pair * 2 + 1, :, zp * 128 : zp * 128 + 128] = jnp.concatenate([a[:, 64:], b[:, 64:]], axis=1)

    def send_piece(p):
        send(piece_out.at[p], pieces.at[f], ss.at[5], rs.at[5], p // NY, z, p % NY, core)

    for i in range(NX):
        if i == 1:
            wait_bytes(slots_b, halves.at[1])
        px = (x + i) % NX
        for j in range(2):
            cut_pair(halves_of[i], px * 2 + j)
        for step in ((2, 1, 3), (0,))[i]:
            send_piece(px * NY + (y + step) % NY)
    local(piece_out.at[f], pieces.at[f], rs.at[5])

    each((2, 6, 1, 7), line_kv)

    @pl.when(core == 1)
    def _():
        pl.semaphore_wait(vouch.at[1], 1)
        greet(vouch.at[3], x, z, y, 0)

    @pl.when(core == 0)
    def _():
        pl.semaphore_wait(vouch.at[3], 1)

    for step in (2, 1, 3):
        send_piece((1 - x) * NY + (y + step) % NY)

    @pl.when(core == 1)
    def _():
        pl.semaphore_wait(vouch.at[2], 2)
        greet(vouch.at[4], x, z, y, 0)

    @pl.when(core == 0)
    def _():
        pl.semaphore_wait(vouch.at[4], 1)

    each((4, 3, 5), line_kv)
    each(LINE, line_q)
    each(LINE, line_w)
    each(LINE, line_cq)

    wait_bytes(kv.at[0], rs.at[1])
    for t in (2, 1, 3):
        send(kv.at[y], kv.at[y], ss.at[6], kv_rs.at[t - 1], x, z, (y + t) % NY, core)
    wait_bytes(queries.at[0], rs.at[2])
    for t in (2, 1, 3):
        p = (xc + t) % (NX * NC)
        send(queries.at[xc], queries.at[xc], ss.at[7], rs.at[6], p // NC, z, y, p % NC)

    wait_bytes(pieces, rs.at[5])
    piece = pieces[(owner // (NC * NY * NZ)) * NY + (owner // NC) % NY]
    for r in range(4):
        for c in range(2):
            sub_out[r * 2 + c] = piece[r * 16 : r * 16 + 16, c * 256 : c * 256 + 256]

    def line_subs(t):
        zz = (z + t) % NZ
        send(sub_out.at[zz], subs.at[z], ss.at[8], rs.at[7], x, zz, y, core)

    each(LINE, line_subs)
    local(sub_out.at[z], subs.at[z], rs.at[7])

    wait_bytes(weight.at[:, :, 0], rs.at[4])
    send(weight.at[:, :, core], weight.at[:, :, core], ss.at[14], rs.at[9], x, z, y, other)

    wait_bytes(subs, rs.at[7])
    sub_mine[...] = subs[(owner // (NC * NY)) % NZ]
    my_sub = prompt.at[z % 2, rows((z // 2) * 16, 16), :]

    def line_prompt(t):
        send(sub_mine, my_sub, ss.at[11], rs.at[8], x, (z + t) % NZ, y, core)

    each(LINE, line_prompt)
    local(sub_mine, my_sub, rs.at[8])

    for t in range(1, NY):
        wait_bytes(kv.at[0], kv_rs.at[t - 1])
    wait_bytes(queries.at[pl.ds(0, 3)], rs.at[6])

    def self_part(s):
        keys = kv[:, 0].reshape(NY * SLOT, HEAD_DIM)
        values = kv[:, 1].reshape(NY * SLOT, HEAD_DIM)
        scores = dot_last(keys, queries[s])
        top = jnp.max(scores, axis=0, keepdims=True)
        weights = jnp.exp2((scores - top) * SCALE)
        total = jnp.sum(weights, axis=0, keepdims=True)
        acc = dot_first(values, weights.astype(BF16)) * (1.0 / total)
        return acc.astype(BF16), top, total

    for t in (2, 1, 3):
        p = (xc + t) % (NX * NC)
        acc, top, total = self_part(p)
        acc_out[p] = acc
        stat_out[p, 0:1, :] = top
        stat_out[p, 1:2, :] = total
        send(acc_out.at[p], accs.at[xc], ss.at[9], acc_rs.at[t - 1], p // NC, z, y, p % NC)
        send(stat_out.at[p], stats.at[xc], ss.at[10], stat_rs.at[t - 1], p // NC, z, y, p % NC)

    wait_bytes(weight.at[:, :, 0], rs.at[9])
    wait_bytes(prompt, rs.at[8])
    for j in range(2):
        columns = weight[j].reshape(512, HEAD_DIM)
        part = jnp.dot(prompt[0], columns[:256], preferred_element_type=F32)
        part = part + jnp.dot(prompt[1], columns[256:], preferred_element_type=F32)
        part_out[:, j] = part.reshape(PLANE, 8, HEAD_DIM)

    def plane_parts(t):
        px, py = (x + t // NY) % NX, (y + t) % NY
        p = px * NY + py
        send(part_out.at[p], parts.at[f], ss.at[12], rs.at[10], px, z, py, core)

    each(ACROSS, plane_parts)
    parts[f] = part_out[f]

    acc, top, total = self_part(xc)
    accs[xc] = acc
    stats[xc, 0:1, :] = top
    stats[xc, 1:2, :] = total

    wait_bytes(parts.at[pl.ds(0, 7)], rs.at[10])
    cross_kv[core, f] = jnp.sum(parts[...], axis=0).reshape(16, HEAD_DIM).astype(BF16)

    def plane_rows(t):
        px, py = (x + t // NY) % NX, (y + t) % NY
        p = px * NY + py
        for c in (core, other):
            send(cross_kv.at[core, f], cross_kv.at[core, f], ss.at[13], rs.at[12], px, z, py, c)

    each(ACROSS, plane_rows)
    send(cross_kv.at[core, f], cross_kv.at[core, f], ss.at[13], rs.at[12], x, z, y, other)

    for t in range(1, NX * NC):
        wait_bytes(accs.at[0], acc_rs.at[t - 1])
        wait_bytes(stats.at[0], stat_rs.at[t - 1])
    tops = [stats[s, 0:1, :] for s in range(NX * NC)]
    top = jnp.maximum(jnp.maximum(tops[0], tops[1]), jnp.maximum(tops[2], tops[3]))
    shares = [stats[s, 1:2, :] * jnp.exp2((tops[s] - top) * SCALE) for s in range(NX * NC)]
    whole = 1.0 / (shares[0] + shares[1] + shares[2] + shares[3])
    mixed[...] = sum(accs[s].astype(F32) * (shares[s] * whole) for s in range(NX * NC)).T

    wait_bytes(cross_q, rs.at[3])
    wait_bytes(cross_q.at[pl.ds(0, 240), :], rs.at[12])
    cross = cross_kv[...].astype(F32)
    cross_keys = cross[:, :, :8].reshape(NC * HALF, HEAD_DIM).astype(BF16)
    cross_values = cross[:, :, 8:].reshape(NC * HALF, HEAD_DIM).astype(BF16)
    cross_values = cross_values.T
    valid = lax.broadcasted_iota(jnp.int32, (NC * HALF, 4 * TOK), 0) < len_ref[0]

    def send_out(t):
        zz = (z + t) % NZ
        send(out_rows.at[rows(zz * TOK, TOK), :], out_ref.at[:, head_columns(z)], ss.at[15], rs.at[11], x, zz, y, core)

    for steps in ((4, 3, 5, 2), (6, 1, 7, 0)):
        places = [rows((z + t) % NZ * TOK, TOK) for t in steps]
        scores = dot_last(cross_keys, jnp.concatenate([cross_q[place, :] for place in places], axis=0))
        scores = jnp.where(valid, scores, -1e30)
        weights = jnp.exp2((scores - jnp.max(scores, axis=0, keepdims=True)) * SCALE)
        total = jnp.sum(weights, axis=0, keepdims=True)
        crossed = jnp.dot(cross_values, weights.astype(BF16), preferred_element_type=F32) * (1.0 / total)
        crossed = crossed.T
        for i, place in enumerate(places):
            out_rows[place, :] = (mixed[place, :] + crossed[i * TOK : (i + 1) * TOK]).astype(BF16)
        for t in steps:
            if t:
                send_out(t)
    local(out_rows.at[rows(z * TOK, TOK), :], out_ref.at[:, head_columns(z)], rs.at[11])

    wait_bytes(slots_a, ss.at[0])
    wait_bytes(kv.at[0, :, pl.ds(0, 224), :], ss.at[1])
    wait_bytes(queries.at[0, pl.ds(0, 224), :], ss.at[2])
    wait_bytes(queries.at[0, pl.ds(0, 224), :], ss.at[3])
    wait_bytes(kv.at[0, :, pl.ds(0, 224), :], ss.at[4])
    wait_bytes(pieces.at[pl.ds(0, 7)], ss.at[5])
    wait_bytes(kv.at[pl.ds(0, 3)], ss.at[6])
    wait_bytes(queries.at[pl.ds(0, 3)], ss.at[7])
    wait_bytes(subs.at[pl.ds(0, 7)], ss.at[8])
    wait_bytes(accs.at[pl.ds(0, 3)], ss.at[9])
    wait_bytes(stats.at[pl.ds(0, 3)], ss.at[10])
    wait_bytes(subs.at[pl.ds(0, 7)], ss.at[11])
    wait_bytes(parts.at[pl.ds(0, 7)], ss.at[12])
    wait_bytes(cross_q.at[pl.ds(0, 240), :], ss.at[13])
    wait_bytes(weight.at[:, :, 0], ss.at[14])
    wait_bytes(cross_q.at[pl.ds(0, 224), :], ss.at[15])
    wait_bytes(out_ref, rs.at[11])


def on_device(queries, keys, values, cross_queries, text_states, cross_kv_weight, owner, prompt_len):
    smem = pl.BlockSpec(memory_space=pltpu.SMEM)
    hbm = pl.BlockSpec(memory_space=pltpu.HBM)
    return pl.pallas_call(
        kernel,
        out_shape=pltpu.VMEM((TOK, HEADS * HEAD_DIM), BF16),
        in_specs=[smem, smem] + [hbm] * 6,
        out_specs=pl.BlockSpec(memory_space=pltpu.VMEM),
        scratch_shapes=[
            pltpu.VMEM((NC, 64, 2048), BF16),
            pltpu.VMEM((NC, 64, 2048), BF16),
            pltpu.VMEM((PLANE, 64, 512), BF16),
            pltpu.VMEM((PLANE, 64, 512), BF16),
            pltpu.VMEM((NZ, 16, 256), BF16),
            pltpu.VMEM((NZ, 16, 256), BF16),
            pltpu.VMEM((16, 256), BF16),
            pltpu.VMEM((2, HALF, 256), BF16),
            pltpu.VMEM((2, NZ, NC, TOK, HEAD_DIM), BF16),
            pltpu.VMEM((NY, 2, SLOT, HEAD_DIM), BF16),
            pltpu.VMEM((NX * NC, SLOT, HEAD_DIM), BF16),
            pltpu.VMEM((SLOT, HEAD_DIM), BF16),
            pltpu.VMEM((PLANE, 2, 8, HEAD_DIM), F32),
            pltpu.VMEM((PLANE, 2, 8, HEAD_DIM), F32),
            pltpu.VMEM((NC, PLANE, 16, HEAD_DIM), BF16),
            pltpu.VMEM((SLOT, HEAD_DIM), F32),
            pltpu.VMEM((NX * NC, HEAD_DIM, SLOT), BF16),
            pltpu.VMEM((NX * NC, HEAD_DIM, SLOT), BF16),
            pltpu.VMEM((NX * NC, 8, SLOT), F32),
            pltpu.VMEM((NX * NC, 8, SLOT), F32),
            pltpu.VMEM((SLOT, HEAD_DIM), BF16),
            pltpu.SemaphoreType.DMA((16,)),
            pltpu.SemaphoreType.DMA((13,)),
            pltpu.SemaphoreType.DMA((NY - 1,)),
            pltpu.SemaphoreType.DMA((NX * NC - 1,)),
            pltpu.SemaphoreType.DMA((NX * NC - 1,)),
            pltpu.SemaphoreType.REGULAR((5,)),
            pltpu.SemaphoreType.DMA((NX,)),
        ],
        compiler_params=pltpu.CompilerParams(
            collective_id=0, has_side_effects=True, vmem_limit_bytes=56 * 1024 * 1024
        ),
        cost_estimate=pl.CostEstimate(flops=700_000_000, bytes_accessed=2_000_000, transcendentals=1_100_000),
    )(owner, prompt_len, queries, keys, values, cross_queries, text_states, cross_kv_weight)


def solution(mesh):
    return jax.shard_map(
        on_device,
        mesh=mesh,
        in_specs=(
            P(("batch", "seq"), None),
            P(("batch", "seq"), None),
            P(("batch", "seq"), None),
            P(("batch", "seq"), None),
            P(("batch", "seq"), None, None),
            P("seq", None),
            P("batch"),
            P("batch"),
        ),
        out_specs=P(("batch", "seq"), None),
        check_vma=False,
    )
```

```python
import math

import jax
import jax.numpy as jnp
from jax import lax
from jax.experimental import pallas as pl
from jax.experimental.pallas import tpu as pltpu
from jax.sharding import PartitionSpec as P

HEAD_DIM = 128
HEADS = 8
NX, NZ, NY, NC = 2, 8, 4, 2
PLANE = NX * NY
TOK = 32
SLOT = TOK * NZ
SCALE = math.log2(math.e) / math.sqrt(HEAD_DIM)
HALF = 64
LINE = (4, 3, 5, 2, 6, 1, 7)
ACROSS = (6, 5, 7, 2, 4, 1, 3)
F32 = jnp.float32
BF16 = jnp.bfloat16


def index_of(x, z, y, core):
    return ((x * NZ + z) * NY + y) * NC + core


def send(src, dst, send_sem, recv_sem, x, z, y, core):
    pltpu.make_async_remote_copy(
        src_ref=src,
        dst_ref=dst,
        send_sem=send_sem,
        recv_sem=recv_sem,
        device_id={"seq": index_of(x, z, y, core)},
        device_id_type=pl.DeviceIdType.MESH,
    ).start()


def each(steps, fn):
    for t in steps:
        fn(t)


def local(src, dst, sem):
    pltpu.make_async_copy(src, dst, sem).start()


def wait_bytes(ref, sem):
    pltpu.make_async_copy(ref, ref, sem).wait()


def head_columns(head):
    return pl.ds(pl.multiple_of(head * HEAD_DIM, HEAD_DIM), HEAD_DIM)


def half(x, i):
    return pl.ds(pl.multiple_of((x + i) % NX * 2048, 2048), 2048)


def rows(start, count):
    return pl.ds(pl.multiple_of(start, count), count)


def dot_last(a, b):
    return lax.dot_general(a, b, (((1,), (1,)), ((), ())), preferred_element_type=F32)


def dot_first(a, b):
    return lax.dot_general(a, b, (((0,), (0,)), ((), ())), preferred_element_type=F32)


def kernel(
    owner_ref,
    len_ref,
    q_hbm,
    k_hbm,
    v_hbm,
    cq_hbm,
    text_hbm,
    w_hbm,
    out_ref,
    slots_a,
    slots_b,
    piece_out,
    pieces,
    sub_out,
    subs,
    sub_mine,
    prompt,
    weight,
    kv,
    queries,
    cross_q,
    part_out,
    parts,
    cross_kv,
    mixed,
    acc_out,
    accs,
    stat_out,
    stats,
    out_rows,
    ss,
    rs,
    kv_rs,
    acc_rs,
    stat_rs,
    vouch,
    halves,
):
    me = lax.axis_index("seq")
    core = me % NC
    y = (me // NC) % NY
    z = (me // (NC * NY)) % NZ
    x = me // (NC * NY * NZ)
    f = x * NY + y
    xc = x * NC + core
    other = 1 - core
    halves_of = (slots_a, slots_b)

    barrier = pltpu.get_barrier_semaphore()

    def greet(sem, x, z, y, core):
        pl.semaphore_signal(
            sem, inc=1, device_id={"seq": index_of(x, z, y, core)}, device_id_type=pl.DeviceIdType.MESH
        )

    for t in (2, 6, 1, 7):
        greet(barrier, x, (z + t) % NZ, y, 1)
    for t in (2, 1, 3):
        greet(barrier, x, z, (y + t) % NY, 1)
    greet(barrier, 1 - x, z, y, 1)
    greet(barrier, x, z, y, other)
    for i in range(NX):
        local(text_hbm.at[0, rows(core * 64, 64), half(x, i)], halves_of[i].at[core], halves.at[i])

    @pl.when(core == 0)
    def _():
        pl.semaphore_wait(barrier, 1)

    @pl.when(core == 1)
    def _():
        pl.semaphore_wait(barrier, 17)

    @pl.when(core == 1)
    def _():
        greet(vouch.at[0], x, z, y, 0)
        greet(vouch.at[1], 1 - x, z, y, 1)
        for t in (2, 6):
            greet(vouch.at[2], x, (z + t) % NZ, y, 1)

    theirs = rows(other * 64, 64)
    for i in range(NX):
        columns = half(x, i)
        send(text_hbm.at[0, theirs, columns], halves_of[i].at[core], ss.at[0], halves.at[i], x, z, y, other)

    def line_kv(t):
        zz = (z + t) % NZ
        send(k_hbm.at[:, head_columns(zz)], kv.at[y, 0, rows(z * TOK, TOK), :], ss.at[1], rs.at[1], x, zz, y, core)
        send(v_hbm.at[:, head_columns(zz)], kv.at[y, 1, rows(z * TOK, TOK), :], ss.at[1], rs.at[1], x, zz, y, core)

    def line_q(t):
        zz = (z + t) % NZ
        send(q_hbm.at[:, head_columns(zz)], queries.at[xc, rows(z * TOK, TOK), :], ss.at[2], rs.at[2], x, zz, y, core)

    def line_cq(t):
        zz = (z + t) % NZ
        send(cq_hbm.at[:, head_columns(zz)], cross_q.at[rows(z * TOK, TOK), :], ss.at[3], rs.at[3], x, zz, y, core)

    def line_w(t):
        zz = (z + t) % NZ
        for j in range(2):
            send(w_hbm.at[:, head_columns(j * HEADS + zz)], weight.at[j, z, core], ss.at[4], rs.at[4], x, zz, y, core)

    @pl.when(core == 0)
    def _():
        pl.semaphore_wait(vouch.at[0], 1)

    owner = owner_ref[0]
    owner_core = owner % NC
    wait_bytes(slots_a, halves.at[0])

    def cut_pair(slots, pair):
        for zp in range(NZ // 2):
            base = pl.multiple_of(pair % 2 * 128 + zp * 512, 128)
            a = slots[owner_core, :, pl.ds(base, 128)]
            b = slots[owner_core, :, pl.ds(pl.multiple_of(base + 256, 128), 128)]
            piece_out[pair * 2, :, zp * 128 : zp * 128 + 128] = jnp.concatenate([a[:, :64], b[:, :64]], axis=1)
            piece_out[pair * 2 + 1, :, zp * 128 : zp * 128 + 128] = jnp.concatenate([a[:, 64:], b[:, 64:]], axis=1)

    def send_piece(p):
        send(piece_out.at[p], pieces.at[f], ss.at[5], rs.at[5], p // NY, z, p % NY, core)

    for i in range(NX):
        if i == 1:
            wait_bytes(slots_b, halves.at[1])
        px = (x + i) % NX
        for j in range(2):
            cut_pair(halves_of[i], px * 2 + j)
        for step in ((2, 1, 3), (0,))[i]:
            send_piece(px * NY + (y + step) % NY)
    local(piece_out.at[f], pieces.at[f], rs.at[5])

    local(k_hbm.at[:, head_columns(z)], kv.at[y, 0, rows(z * TOK, TOK), :], rs.at[1])
    local(v_hbm.at[:, head_columns(z)], kv.at[y, 1, rows(z * TOK, TOK), :], rs.at[1])
    local(q_hbm.at[:, head_columns(z)], queries.at[xc, rows(z * TOK, TOK), :], rs.at[2])
    local(cq_hbm.at[:, head_columns(z)], cross_q.at[rows(z * TOK, TOK), :], rs.at[3])
    for j in range(2):
        local(w_hbm.at[:, head_columns(j * HEADS + z)], weight.at[j, z, core], rs.at[4])

    each((2, 6, 1, 7), line_kv)

    @pl.when(core == 1)
    def _():
        pl.semaphore_wait(vouch.at[1], 1)
        greet(vouch.at[3], x, z, y, 0)

    @pl.when(core == 0)
    def _():
        pl.semaphore_wait(vouch.at[3], 1)

    for step in (2, 1, 3):
        send_piece((1 - x) * NY + (y + step) % NY)

    @pl.when(core == 1)
    def _():
        pl.semaphore_wait(vouch.at[2], 2)
        greet(vouch.at[4], x, z, y, 0)

    @pl.when(core == 0)
    def _():
        pl.semaphore_wait(vouch.at[4], 1)

    each((4, 3, 5), line_kv)
    each(LINE, line_q)
    each(LINE, line_w)

    wait_bytes(kv.at[0], rs.at[1])
    for t in (2, 1, 3):
        send(kv.at[y], kv.at[y], ss.at[6], kv_rs.at[t - 1], x, z, (y + t) % NY, core)
    wait_bytes(queries.at[0], rs.at[2])
    for t in (2, 1, 3):
        p = (xc + t) % (NX * NC)
        send(queries.at[xc], queries.at[xc], ss.at[7], rs.at[6], p // NC, z, y, p % NC)

    wait_bytes(pieces, rs.at[5])
    piece = pieces[(owner // (NC * NY * NZ)) * NY + (owner // NC) % NY]
    for r in range(4):
        for c in range(2):
            sub_out[r * 2 + c] = piece[r * 16 : r * 16 + 16, c * 256 : c * 256 + 256]

    def line_subs(t):
        zz = (z + t) % NZ
        send(sub_out.at[zz], subs.at[z], ss.at[8], rs.at[7], x, zz, y, core)

    each(LINE, line_subs)
    local(sub_out.at[z], subs.at[z], rs.at[7])

    wait_bytes(weight.at[:, :, 0], rs.at[4])
    send(weight.at[:, :, core], weight.at[:, :, core], ss.at[14], rs.at[9], x, z, y, other)

    wait_bytes(subs, rs.at[7])
    sub_mine[...] = subs[(owner // (NC * NY)) % NZ]
    my_sub = prompt.at[z % 2, rows((z // 2) * 16, 16), :]

    def line_prompt(t):
        send(sub_mine, my_sub, ss.at[11], rs.at[8], x, (z + t) % NZ, y, core)

    each(LINE, line_prompt)
    local(sub_mine, my_sub, rs.at[8])

    for t in range(1, NY):
        wait_bytes(kv.at[0], kv_rs.at[t - 1])
    wait_bytes(queries.at[pl.ds(0, 3)], rs.at[6])

    def self_part(s):
        keys = kv[:, 0].reshape(NY * SLOT, HEAD_DIM)
        values = kv[:, 1].reshape(NY * SLOT, HEAD_DIM)
        scores = dot_last(keys, queries[s])
        top = jnp.max(scores, axis=0, keepdims=True)
        weights = jnp.exp2((scores - top) * SCALE)
        total = jnp.sum(weights, axis=0, keepdims=True)
        acc = dot_first(values, weights.astype(BF16)) * (1.0 / total)
        return acc.astype(BF16), top, total

    for t in (2, 1, 3):
        p = (xc + t) % (NX * NC)
        acc, top, total = self_part(p)
        acc_out[p] = acc
        stat_out[p, 0:1, :] = top
        stat_out[p, 1:2, :] = total
        send(acc_out.at[p], accs.at[xc], ss.at[9], acc_rs.at[t - 1], p // NC, z, y, p % NC)
        send(stat_out.at[p], stats.at[xc], ss.at[10], stat_rs.at[t - 1], p // NC, z, y, p % NC)

    wait_bytes(weight.at[:, :, 0], rs.at[9])
    wait_bytes(prompt, rs.at[8])
    for j in range(2):
        columns = weight[j].reshape(512, HEAD_DIM)
        part = jnp.dot(prompt[0], columns[:256], preferred_element_type=F32)
        part = part + jnp.dot(prompt[1], columns[256:], preferred_element_type=F32)
        part_out[:, j] = part.reshape(PLANE, 8, HEAD_DIM)

    def plane_parts(t):
        px, py = (x + t // NY) % NX, (y + t) % NY
        p = px * NY + py
        send(part_out.at[p], parts.at[f], ss.at[12], rs.at[10], px, z, py, core)

    each(ACROSS, plane_parts)
    each(LINE, line_cq)
    parts[f] = part_out[f]

    acc, top, total = self_part(xc)
    accs[xc] = acc
    stats[xc, 0:1, :] = top
    stats[xc, 1:2, :] = total

    wait_bytes(parts.at[pl.ds(0, 7)], rs.at[10])
    cross_kv[core, f] = jnp.sum(parts[...], axis=0).reshape(16, HEAD_DIM).astype(BF16)

    def plane_rows(t):
        px, py = (x + t // NY) % NX, (y + t) % NY
        p = px * NY + py
        for c in (core, other):
            send(cross_kv.at[core, f], cross_kv.at[core, f], ss.at[13], rs.at[12], px, z, py, c)

    each(ACROSS, plane_rows)
    send(cross_kv.at[core, f], cross_kv.at[core, f], ss.at[13], rs.at[12], x, z, y, other)

    for t in range(1, NX * NC):
        wait_bytes(accs.at[0], acc_rs.at[t - 1])
        wait_bytes(stats.at[0], stat_rs.at[t - 1])
    tops = [stats[s, 0:1, :] for s in range(NX * NC)]
    top = jnp.maximum(jnp.maximum(tops[0], tops[1]), jnp.maximum(tops[2], tops[3]))
    shares = [stats[s, 1:2, :] * jnp.exp2((tops[s] - top) * SCALE) for s in range(NX * NC)]
    whole = 1.0 / (shares[0] + shares[1] + shares[2] + shares[3])
    mixed[...] = sum(accs[s].astype(F32) * (shares[s] * whole) for s in range(NX * NC)).T

    wait_bytes(cross_q, rs.at[3])
    wait_bytes(cross_q.at[pl.ds(0, 240), :], rs.at[12])
    cross = cross_kv[...].astype(F32)
    cross_keys = cross[:, :, :8].reshape(NC * HALF, HEAD_DIM).astype(BF16)
    cross_values = cross[:, :, 8:].reshape(NC * HALF, HEAD_DIM).astype(BF16)
    cross_values = cross_values.T
    valid = lax.broadcasted_iota(jnp.int32, (NC * HALF, 4 * TOK), 0) < len_ref[0]

    def send_out(t):
        zz = (z + t) % NZ
        send(out_rows.at[rows(zz * TOK, TOK), :], out_ref.at[:, head_columns(z)], ss.at[15], rs.at[11], x, zz, y, core)

    for steps in ((4, 3, 5, 2), (6, 1, 7, 0)):
        places = [rows((z + t) % NZ * TOK, TOK) for t in steps]
        scores = dot_last(cross_keys, jnp.concatenate([cross_q[place, :] for place in places], axis=0))
        scores = jnp.where(valid, scores, -1e30)
        weights = jnp.exp2((scores - jnp.max(scores, axis=0, keepdims=True)) * SCALE)
        total = jnp.sum(weights, axis=0, keepdims=True)
        crossed = jnp.dot(cross_values, weights.astype(BF16), preferred_element_type=F32) * (1.0 / total)
        crossed = crossed.T
        for i, place in enumerate(places):
            out_rows[place, :] = (mixed[place, :] + crossed[i * TOK : (i + 1) * TOK]).astype(BF16)
        for t in steps:
            if t:
                send_out(t)
    local(out_rows.at[rows(z * TOK, TOK), :], out_ref.at[:, head_columns(z)], rs.at[11])

    wait_bytes(slots_a, ss.at[0])
    wait_bytes(kv.at[0, :, pl.ds(0, 224), :], ss.at[1])
    wait_bytes(queries.at[0, pl.ds(0, 224), :], ss.at[2])
    wait_bytes(queries.at[0, pl.ds(0, 224), :], ss.at[3])
    wait_bytes(kv.at[0, :, pl.ds(0, 224), :], ss.at[4])
    wait_bytes(pieces.at[pl.ds(0, 7)], ss.at[5])
    wait_bytes(kv.at[pl.ds(0, 3)], ss.at[6])
    wait_bytes(queries.at[pl.ds(0, 3)], ss.at[7])
    wait_bytes(subs.at[pl.ds(0, 7)], ss.at[8])
    wait_bytes(accs.at[pl.ds(0, 3)], ss.at[9])
    wait_bytes(stats.at[pl.ds(0, 3)], ss.at[10])
    wait_bytes(subs.at[pl.ds(0, 7)], ss.at[11])
    wait_bytes(parts.at[pl.ds(0, 7)], ss.at[12])
    wait_bytes(cross_q.at[pl.ds(0, 240), :], ss.at[13])
    wait_bytes(weight.at[:, :, 0], ss.at[14])
    wait_bytes(cross_q.at[pl.ds(0, 224), :], ss.at[15])
    wait_bytes(out_ref, rs.at[11])


def on_device(queries, keys, values, cross_queries, text_states, cross_kv_weight, owner, prompt_len):
    smem = pl.BlockSpec(memory_space=pltpu.SMEM)
    hbm = pl.BlockSpec(memory_space=pltpu.HBM)
    return pl.pallas_call(
        kernel,
        out_shape=pltpu.VMEM((TOK, HEADS * HEAD_DIM), BF16),
        in_specs=[smem, smem] + [hbm] * 6,
        out_specs=pl.BlockSpec(memory_space=pltpu.VMEM),
        scratch_shapes=[
            pltpu.VMEM((NC, 64, 2048), BF16),
            pltpu.VMEM((NC, 64, 2048), BF16),
            pltpu.VMEM((PLANE, 64, 512), BF16),
            pltpu.VMEM((PLANE, 64, 512), BF16),
            pltpu.VMEM((NZ, 16, 256), BF16),
            pltpu.VMEM((NZ, 16, 256), BF16),
            pltpu.VMEM((16, 256), BF16),
            pltpu.VMEM((2, HALF, 256), BF16),
            pltpu.VMEM((2, NZ, NC, TOK, HEAD_DIM), BF16),
            pltpu.VMEM((NY, 2, SLOT, HEAD_DIM), BF16),
            pltpu.VMEM((NX * NC, SLOT, HEAD_DIM), BF16),
            pltpu.VMEM((SLOT, HEAD_DIM), BF16),
            pltpu.VMEM((PLANE, 2, 8, HEAD_DIM), F32),
            pltpu.VMEM((PLANE, 2, 8, HEAD_DIM), F32),
            pltpu.VMEM((NC, PLANE, 16, HEAD_DIM), BF16),
            pltpu.VMEM((SLOT, HEAD_DIM), F32),
            pltpu.VMEM((NX * NC, HEAD_DIM, SLOT), BF16),
            pltpu.VMEM((NX * NC, HEAD_DIM, SLOT), BF16),
            pltpu.VMEM((NX * NC, 8, SLOT), F32),
            pltpu.VMEM((NX * NC, 8, SLOT), F32),
            pltpu.VMEM((SLOT, HEAD_DIM), BF16),
            pltpu.SemaphoreType.DMA((16,)),
            pltpu.SemaphoreType.DMA((13,)),
            pltpu.SemaphoreType.DMA((NY - 1,)),
            pltpu.SemaphoreType.DMA((NX * NC - 1,)),
            pltpu.SemaphoreType.DMA((NX * NC - 1,)),
            pltpu.SemaphoreType.REGULAR((5,)),
            pltpu.SemaphoreType.DMA((NX,)),
        ],
        compiler_params=pltpu.CompilerParams(
            collective_id=0, has_side_effects=True, vmem_limit_bytes=56 * 1024 * 1024
        ),
        cost_estimate=pl.CostEstimate(flops=700_000_000, bytes_accessed=2_000_000, transcendentals=1_100_000),
    )(owner, prompt_len, queries, keys, values, cross_queries, text_states, cross_kv_weight)


def solution(mesh):
    return jax.shard_map(
        on_device,
        mesh=mesh,
        in_specs=(
            P(("batch", "seq"), None),
            P(("batch", "seq"), None),
            P(("batch", "seq"), None),
            P(("batch", "seq"), None),
            P(("batch", "seq"), None, None),
            P("seq", None),
            P("batch"),
            P("batch"),
        ),
        out_specs=P(("batch", "seq"), None),
        check_vma=False,
    )
```
